32 devices in a mesh: seq: 8 (over z, y), fsdp: 4 (over x, core).
Axes of the slice: x: 2, y: 2, z: 4, core: 2. Of those that a mesh axis runs over, the one named last changes fastest.
Arguments:
- tokens: bfloat16 [8, 1024, 1024], P('fsdp', 'seq'), may hold values from -6 to 6
- doc_bounds: int32 [8, 2], P('fsdp'), may hold values from 1 to 1024, as said below
- w_qkv: bfloat16 [2, 1024, 3072], P(None, ('seq', 'fsdp')), may hold values from -0.1875 to 0.1875
- w_out: bfloat16 [2, 1024, 1024], P(None, ('seq', 'fsdp')), may hold values from -1.5 to 1.5
- w_gate: bfloat16 [2, 1024, 2816], P(None, ('seq', 'fsdp')), may hold values from -0.1875 to 0.1875
- w_up: bfloat16 [2, 1024, 2816], P(None, ('seq', 'fsdp')), may hold values from -0.1875 to 0.1875
- w_down: bfloat16 [2, 2816, 1024], P(None, ('seq', 'fsdp')), may hold values from -0.109375 to 0.109375
- norm_attn: bfloat16 [2, 1024], P(None, ('seq', 'fsdp')), may hold values from 0.5 to 1.5
- norm_mlp: bfloat16 [2, 1024], P(None, ('seq', 'fsdp')), may hold values from 0.5 to 1.5
- out_grad: bfloat16 [8, 1024, 1024], P('fsdp', 'seq'), may hold values from -6 to 6
Outputs:
- hidden_out: float32 [8, 1024, 1024], P('fsdp', 'seq')
- in_grad: float32 [8, 1024, 1024], P('fsdp', 'seq')
- grad_qkv: float32 [2, 1024, 3072], P(None, ('seq', 'fsdp'))
- grad_out: float32 [2, 1024, 1024], P(None, ('seq', 'fsdp'))
- grad_gate: float32 [2, 1024, 2816], P(None, ('seq', 'fsdp'))
- grad_up: float32 [2, 1024, 2816], P(None, ('seq', 'fsdp'))
- grad_down: float32 [2, 2816, 1024], P(None, ('seq', 'fsdp'))
- grad_norm_attn: float32 [2, 1024], P(None, ('seq', 'fsdp'))
- grad_norm_mlp: float32 [2, 1024], P(None, ('seq', 'fsdp'))
- v1_grad: float32 [8, 1024, 1024], P('fsdp', 'seq')
The draws below stay inside these ranges and needn't reach their ends.
Inputs may be any that keep to these rules, and one draw needn't show every extreme that they name: `doc_bounds`: per slot, column 0 is the first position of the slot's long document, 1 to 64; positions before it form a short document. Column 1 is the end of the valid tokens, 897 to 1024; positions from it on are padding.
All inputs are finite; a program needn't handle non-finite values.
Results may differ from the reference program's by a relative error of at most 0.033.
Values may be sent and summed in bfloat16 or wider, within the bound.
No kernel may reach another device: no remote copies, remote signals or barrier semaphores. Data moves between devices by JAX's collectives and lax.ppermute only.
A program may use at most 384 MiB of HBM per device.

```python
import jax
import jax.numpy as jnp
from jax import lax

D = 1024
H = 16
HD = 64
FF = 2816
LAYERS = 2
TOK_DEV = 128
SEQ_LEN = 1024
SLOTS = 8


def draw_doc_bounds(key, part):
    key = jax.random.fold_in(key, 11)
    first_key, second_key, third_key, fourth_key = jax.random.split(key, 4)
    half_size = TOK_DEV // 2
    starts = jax.random.randint(first_key, (SLOTS,), 1, half_size + 1)
    order_one = jax.random.permutation(second_key, SLOTS)
    starts = jnp.where(order_one == 0, 1, jnp.where(order_one == 1, half_size, starts))
    lowest_end = SEQ_LEN - TOK_DEV + 1
    ends = jax.random.randint(third_key, (SLOTS,), lowest_end, SEQ_LEN + 1)
    order_two = jax.random.permutation(fourth_key, SLOTS)
    ends = jnp.where(order_two == 0, lowest_end, jnp.where(order_two == 1, SEQ_LEN, ends))
    return jnp.stack([starts, ends], axis=1).astype(jnp.int32)


def block_levels(stream_key, shape, shards, smallest, largest):
    def one(position, shards_of):
        steps = jax.random.uniform(jax.random.fold_in(jax.random.fold_in(stream_key, 6), position), (shards_of,), jnp.float32, smallest / len(shards), largest / len(shards))
        return jnp.repeat(jnp.exp(steps), shape[position] // shards_of).reshape((-1,) + (1,) * (len(shape) - position - 1))

    level = one(*shards[0])
    for cut in shards[1:]:
        level = level * one(*cut)
    return level


def gaussian(stream_key, dims, scale, most, cuts=(), held_as=jnp.bfloat16):
    factor_of = block_levels(stream_key, dims, cuts, -0.22, 0.18) if cuts else 1.0
    values = jax.random.normal(stream_key, dims, jnp.float32) * scale * factor_of
    return jnp.minimum(jnp.maximum(values, -most), most).astype(held_as)


def setup_inputs(seed: int = 0) -> dict:
    key_list = jax.random.split(jax.random.key(seed), 11)
    tokens = gaussian(key_list[0], (SLOTS, SEQ_LEN, D), 1.0, 6.0, ((0, 4), (1, 8)))
    doc_bounds = draw_doc_bounds(jax.random.fold_in(key_list[10], 71), 0)
    w_qkv = gaussian(key_list[2], (LAYERS, D, 3 * D), D ** -0.5, 0.1875, ((1, 32),))
    w_out = gaussian(key_list[3], (LAYERS, D, D), (max(D // 64, 1)) ** -0.5, 1.5, ((1, 32),))
    w_gate = gaussian(key_list[4], (LAYERS, D, FF), D ** -0.5, 0.1875, ((1, 32),))
    w_up = gaussian(key_list[5], (LAYERS, D, FF), D ** -0.5, 0.1875, ((1, 32),))
    w_down = gaussian(key_list[6], (LAYERS, FF, D), FF ** -0.5, 0.109375, ((1, 32),))
    norm_attn = jnp.clip(1.0 + 0.1 * jax.random.normal(key_list[7], (LAYERS, D), jnp.float32), 0.5, 1.5).astype(jnp.bfloat16)
    norm_mlp = jnp.clip(1.0 + 0.1 * jax.random.normal(key_list[8], (LAYERS, D), jnp.float32), 0.5, 1.5).astype(jnp.bfloat16)
    out_grad = gaussian(key_list[9], (SLOTS, SEQ_LEN, D), 1.0, 6.0, ((0, 4), (1, 8)))
    return dict(tokens=tokens, doc_bounds=doc_bounds, w_qkv=w_qkv, w_out=w_out, w_gate=w_gate, w_up=w_up, w_down=w_down, norm_attn=norm_attn, norm_mlp=norm_mlp, out_grad=out_grad)


@jax.custom_vjp
def low(v):
    return lax.optimization_barrier(v.astype(jnp.bfloat16)).astype(jnp.float32)

@jax.custom_vjp
def low_back(v):
    return v

def low_keep(v):
    return (low(v), None)

def low_pass(kept, grad):
    return (grad,)

def back_keep(v):
    return (v, None)

def back_low(kept, grad):
    return (low(grad),)
low.defvjp(low_keep, low_pass)
low_back.defvjp(back_keep, back_low)
epsilon = 1e-05
masked_score = -1e+30
highest = lax.Precision.HIGHEST

def labels(position_index, bounds_row):
    start_at = bounds_row[0]
    end_at = bounds_row[1]
    segment = jnp.where(position_index < start_at, 0, jnp.where(position_index < end_at, 1, 2)).astype(jnp.int32)
    doc_base = jnp.where(position_index < start_at, 0, jnp.where(position_index < end_at, start_at, end_at))
    return (segment, (position_index - doc_base).astype(jnp.int32))

def rotary(positions):
    frequency = 10000.0 ** (-jnp.arange(HD // 2, dtype=jnp.float32) * 2.0 / HD)
    angles = positions.astype(jnp.float32)[:, None] * frequency[None, :]
    return (jnp.cos(angles)[:, None, :], jnp.sin(angles)[:, None, :])

def rotate(rows_in, cosine_table, sine_table):
    half_size = rows_in.shape[-1] // 2
    first_half = rows_in[..., :half_size]
    second_half = rows_in[..., half_size:]
    return jnp.concatenate([first_half * cosine_table - second_half * sine_table, second_half * cosine_table + first_half * sine_table], axis=-1)

def rms_gain(hidden, gain_row):
    return hidden * lax.rsqrt(lax.optimization_barrier(jnp.mean(hidden * hidden, axis=-1, keepdims=True)) + epsilon) * gain_row

def attend(queries, key_rows, value_rows, segment):
    total_rows = queries.shape[0]
    block_rows = min(512, total_rows)
    key_index = jnp.arange(total_rows, dtype=jnp.int32)

    def one_block(anchor):
        query_block = lax.dynamic_slice_in_dim(queries, anchor, block_rows, 0)
        query_index = anchor + jnp.arange(block_rows, dtype=jnp.int32)
        query_segment = lax.dynamic_slice_in_dim(segment, anchor, block_rows, 0)
        raw_scores = low_back(jnp.einsum('qhd,khd->qhk', query_block, key_rows, precision=highest))
        allowed = ((key_index[None, :] <= query_index[:, None]) & (segment[None, :] == query_segment[:, None]))[:, None, :]
        scores = jnp.where(allowed, raw_scores * 0.125, masked_score)
        row_max = lax.optimization_barrier(jnp.max(scores, axis=-1, keepdims=True))
        weights = jnp.where(allowed, jnp.exp(scores - row_max), 0.0)
        probability = weights / lax.optimization_barrier(jnp.sum(weights, axis=-1, keepdims=True))
        return jnp.einsum('qhk,khd->qhd', low(probability), value_rows, precision=highest)
    anchors = jnp.arange(total_rows // block_rows, dtype=jnp.int32) * block_rows
    blocks = lax.map(jax.checkpoint(one_block), anchors)
    return blocks.reshape(total_rows, queries.shape[1], queries.shape[2])

def layer(hidden, weights, cosine_table, sine_table, segment, shift_rows, first_values):
    qkv_w, out_w, gate_w, up_w, down_w, attn_gain, mlp_gain = weights
    total_rows = hidden.shape[0]
    attn_in = low(rms_gain(hidden, attn_gain))
    projected = low_back(jnp.dot(attn_in, qkv_w, precision=highest))
    queries = low(rotate(projected[:, :D].reshape(total_rows, H, HD), cosine_table, sine_table))
    key_rows = low(rotate(projected[:, D:2 * D].reshape(total_rows, H, HD), cosine_table, sine_table))
    own_values = projected[:, 2 * D:]
    if first_values is None:
        own_values = own_values + shift_rows
        blended = own_values
    else:
        blended = 0.5 * own_values + 0.5 * first_values
    value_rows = low(blended).reshape(total_rows, H, HD)
    attended = low_back(low(attend(queries, key_rows, value_rows, segment).reshape(total_rows, D)))
    middle = hidden + low_back(jnp.dot(attended, out_w, precision=highest))
    mlp_in = low(rms_gain(middle, mlp_gain))
    gate_pre = low_back(jnp.dot(mlp_in, gate_w, precision=highest))
    up_pre = low_back(jnp.dot(mlp_in, up_w, precision=highest))
    activated = low(jax.nn.silu(gate_pre) * up_pre)
    return (middle + low_back(jnp.dot(activated, down_w, precision=highest)), own_values)

def forward(tokens, w_qkv, w_out, w_gate, w_up, w_down, norm_attn, norm_mlp, shift, doc_bounds):

    def per_slot(slot_items):
        hidden, shift_rows, bounds_row = slot_items
        position_index = jnp.arange(SEQ_LEN, dtype=jnp.int32)
        segment, positions = labels(position_index, bounds_row)
        cosine_table, sine_table = rotary(positions)
        first_values = None
        for layer_number in range(LAYERS):
            weights = (w_qkv[layer_number], w_out[layer_number], w_gate[layer_number], w_up[layer_number], w_down[layer_number], norm_attn[layer_number], norm_mlp[layer_number])
            hidden, own_values = layer(hidden, weights, cosine_table, sine_table, segment, shift_rows, first_values)
            if first_values is None:
                first_values = own_values
        return hidden * (segment < 2).astype(jnp.float32)[:, None]
    return lax.map(per_slot, (tokens, shift, doc_bounds))

def reference(tokens, doc_bounds, w_qkv, w_out, w_gate, w_up, w_down, norm_attn, norm_mlp, out_grad):
    floats = tuple((argument.astype(jnp.float32) for argument in (tokens, w_qkv, w_out, w_gate, w_up, w_down, norm_attn, norm_mlp)))
    shift = jnp.zeros(floats[0].shape, jnp.float32)

    def wrapped(hidden, qkv_w, out_w, gate_w, up_w, down_w, attn_gain, mlp_gain, shift_rows):
        return forward(hidden, qkv_w, out_w, gate_w, up_w, down_w, attn_gain, mlp_gain, shift_rows, doc_bounds)
    result, pull_back = jax.vjp(wrapped, floats[0], floats[1], floats[2], floats[3], floats[4], floats[5], floats[6], floats[7], shift)
    grads = pull_back(out_grad.astype(jnp.float32))
    return (result, grads[0], grads[1], grads[2], grads[3], grads[4], grads[5], grads[6], grads[7], grads[8])
```

```python
import functools

import jax
import jax.numpy as jnp
from jax import lax
from jax.experimental import pallas as pl
from jax.experimental.pallas import tpu as pltpu
from jax.sharding import Mesh, PartitionSpec as P

HD = 64
LAYERS = 2
epsilon = 1e-05
masked_score = -1e30
bf16 = jnp.bfloat16
f32 = jnp.float32

ALL = ("sz", "sy", "fx", "fc")
SWAP = ((0, 1), (1, 0))
VMEM_LIMIT = 48 * 1024 * 1024


def dot(left, right):
    return jnp.dot(left, right, preferred_element_type=f32)


def dot_rows(left, right):
    return lax.dot_general(left, right, (((0,), (0,)), ((), ())), preferred_element_type=f32)


def dot_cols(left, right):
    return lax.dot_general(left, right, (((1,), (1,)), ((), ())), preferred_element_type=f32)


def swap_core(value):
    return lax.ppermute(value, "fc", SWAP)


def swap_x(value):
    return lax.ppermute(value, "fx", SWAP)


def swap_y(value):
    return lax.ppermute(value, "sy", SWAP)


def pick(array, index, axis=0):
    return lax.dynamic_index_in_dim(array, index, axis, keepdims=False)


def in_order(flag, first, second, axis):
    return jnp.where(
        flag == 0, jnp.stack([first, second], axis), jnp.stack([second, first], axis)
    )


def exchange(pieces):
    fx, fc = lax.axis_index("fx"), lax.axis_index("fc")
    pieces = pieces.reshape((2, 2) + pieces.shape[1:])
    got = swap_x(pick(pieces, 1 - fx))
    both = in_order(fx, pick(pieces, fx), got, 0)
    got = swap_core(pick(both, 1 - fc, 1))
    both = in_order(fc, pick(both, fc, 1), got, 1)
    return both.reshape((4,) + both.shape[2:])


def join_y(own):
    full = in_order(lax.axis_index("sy"), own, swap_y(own), 1)
    return full.reshape(-1, own.shape[-1])


def reduce_rows(grad, rows):
    sy = lax.axis_index("sy")
    grad = grad.reshape(-1, 2, rows, grad.shape[-1])
    got = swap_y(pick(grad, 1 - sy, 1))
    total = (pick(grad, sy, 1).astype(f32) + got.astype(f32)).astype(bf16)
    return lax.psum_scatter(total, "sz", scatter_dimension=0, tiled=False)


def spread(value):
    over = swap_x(value)
    return (
        jnp.concatenate([value, swap_core(value)]),
        jnp.concatenate([over, swap_core(over)]),
    )


def gather_sum(near, far):
    rows = near.shape[0] // 2
    out = far[:rows] + swap_core(far[rows:].astype(bf16)).astype(f32)
    out = swap_x(out.astype(bf16)).astype(f32)
    own = near[:rows] + swap_core(near[rows:].astype(bf16)).astype(f32)
    return own + out


def normalize(hidden):
    inverse = lax.rsqrt(jnp.mean(hidden * hidden, axis=-1, keepdims=True) + epsilon)
    return (hidden * inverse, inverse)


def norm_back(upstream, normed, inverse, gain_row):
    scaled = upstream * gain_row
    inner_mean = jnp.mean(scaled * normed, axis=-1, keepdims=True)
    return (inverse * (scaled - normed * inner_mean), jnp.sum(upstream * normed, axis=0))


def partner(rows):
    lane = lax.broadcasted_iota(jnp.int32, rows.shape, 1)
    return jnp.where(lane % 64 < 32, pltpu.roll(rows, 96, 1), pltpu.roll(rows, 32, 1))


def block_mask(block, rows, start, end):
    shape = (rows, (block + 1) * rows)
    query = block * rows + lax.broadcasted_iota(jnp.int32, (rows, 1), 0)
    lowest = jnp.where(query < start, 0, jnp.where(query < end, start, end))
    key = lax.broadcasted_iota(jnp.int32, shape, 1)
    return (key <= query) & (key >= lowest)


def softmax_rows(scores, allowed):
    scores = jnp.where(allowed, scores * 0.125, masked_score)
    weights = jnp.exp(scores - jnp.max(scores, axis=-1, keepdims=True))
    return weights * (1.0 / jnp.sum(weights, axis=-1, keepdims=True))


def attention_kernel(blend, scalars, cos_ref, sin_ref, *refs):
    if blend:
        part_ref, first_ref, q_ref, k_ref, v_ref, o_ref = refs
    else:
        part_ref, q_ref, k_ref, v_ref, o_ref = refs
    me, start, end = scalars[0], scalars[1], scalars[2]
    total, width = q_ref.shape
    rows = total // 4
    for i in range(4):
        here = slice(i * rows, (i + 1) * rows)
        there = pl.ds(pl.multiple_of((me ^ i) * rows, rows), rows)
        cosine, sine = cos_ref[here, :], sin_ref[here, :]
        for j in range(width // 128):
            for into, at in ((q_ref, 0), (k_ref, width)):
                piece = part_ref[here, at + j * 128 : at + (j + 1) * 128]
                turned = piece * cosine + partner(piece) * sine
                into[there, j * 128 : (j + 1) * 128] = turned.astype(bf16)
        value = part_ref[here, 2 * width : 3 * width]
        if blend:
            value = 0.5 * value + 0.5 * first_ref[here, 2 * width : 3 * width]
        v_ref[there, :] = value.astype(bf16)
    lane = lax.broadcasted_iota(jnp.int32, (rows, 128), 1)
    for b in range(4):
        allowed = block_mask(b, rows, start, end)
        there = pl.ds(pl.multiple_of((me ^ b) * rows, rows), rows)
        for j in range(width // 128):
            columns = slice(j * 128, (j + 1) * 128)
            query = q_ref[b * rows : (b + 1) * rows, columns]
            keys = k_ref[: (b + 1) * rows, columns]
            values = v_ref[: (b + 1) * rows, columns]
            outs = []
            for h in range(2):
                one = jnp.where(lane // 64 == h, query, jnp.zeros_like(query))
                chance = softmax_rows(dot_cols(one, keys), allowed)
                outs.append(dot(chance.astype(bf16), values))
            o_ref[there, columns] = jnp.where(lane < 64, outs[0], outs[1]).astype(bf16)


def attention_back_kernel(last, scalars, cos_ref, sin_ref, *refs):
    if last:
        q_ref, k_ref, v_ref, up_ref, carry_ref, d_ref, dv_ref, dk_sum, dv_sum = refs
    else:
        q_ref, k_ref, v_ref, up_ref, d_ref, dv_ref, dk_sum, dv_sum = refs
    me, start, end = scalars[0], scalars[1], scalars[2]
    total, width = q_ref.shape
    rows = total // 4
    lane = lax.broadcasted_iota(jnp.int32, (rows, 128), 1)
    dk_sum[...] = jnp.zeros_like(dk_sum)
    dv_sum[...] = jnp.zeros_like(dv_sum)
    for b in range(4):
        allowed = block_mask(b, rows, start, end)
        there = pl.ds(pl.multiple_of((me ^ b) * rows, rows), rows)
        upto = slice(0, (b + 1) * rows)
        cosine, sine = cos_ref[there, :], sin_ref[there, :]
        for j in range(width // 128):
            columns = slice(j * 128, (j + 1) * 128)
            query = q_ref[b * rows : (b + 1) * rows, columns]
            keys, values = k_ref[upto, columns], v_ref[upto, columns]
            up = up_ref[there, columns]
            dq, dk, dv = [], [], []
            for h in range(2):
                mine = lane // 64 == h
                one = jnp.where(mine, query, jnp.zeros_like(query))
                one_up = jnp.where(mine, up, jnp.zeros_like(up))
                chance = softmax_rows(dot_cols(one, keys), allowed)
                back = dot_cols(one_up, values)
                delta = jnp.sum(chance * back, axis=-1, keepdims=True)
                score = (chance * (back - delta) * 0.125).astype(bf16)
                dq.append(dot(score, keys))
                dk.append(dot_rows(score, one))
                dv.append(dot_rows(chance.astype(bf16), one_up))
            dk_sum[upto, columns] += dk[0] + dk[1]
            dv_sum[upto, columns] += dv[0] + dv[1]
            dq = jnp.where(lane < 64, dq[0], dq[1])
            d_ref[there, columns] = (dq * cosine - partner(dq) * sine).astype(bf16)
    for b in range(4):
        there = pl.ds(pl.multiple_of((me ^ b) * rows, rows), rows)
        here = slice(b * rows, (b + 1) * rows)
        cosine, sine = cos_ref[there, :], sin_ref[there, :]
        for j in range(width // 128):
            dk = dk_sum[here, j * 128 : (j + 1) * 128]
            dk = dk * cosine - partner(dk) * sine
            d_ref[there, width + j * 128 : width + (j + 1) * 128] = dk.astype(bf16)
        dv = dv_sum[here, :]
        dv = dv + carry_ref[there, :] if last else 0.5 * dv
        dv_ref[there, :] = dv
        d_ref[there, 2 * width : 3 * width] = dv.astype(bf16)


def kernel_call(body, out_shape, operands, scratch=(), flops=0):
    return pl.pallas_call(
        body,
        out_shape=out_shape,
        in_specs=[pl.BlockSpec(memory_space=pltpu.SMEM)]
        + [pl.BlockSpec(memory_space=pltpu.VMEM)] * (len(operands) - 1),
        out_specs=[pl.BlockSpec(memory_space=pltpu.VMEM)] * len(out_shape),
        scratch_shapes=list(scratch),
        compiler_params=pltpu.CompilerParams(vmem_limit_bytes=VMEM_LIMIT),
        cost_estimate=pl.CostEstimate(flops=flops, bytes_accessed=1 << 22, transcendentals=1 << 20),
    )(*operands)


def turn(rows, cosine, sine):
    total, width = rows.shape
    halves = rows.reshape(total, width // HD, 2, HD // 2)
    cosine = cosine[:, :HD].reshape(total, 1, 2, HD // 2)
    sine = sine[:, :HD].reshape(total, 1, 2, HD // 2)
    return (halves * cosine + halves[:, :, ::-1] * sine).reshape(total, width)


class Attention:
    def __init__(self, me, part, parts, total, bounds):
        self.parts, self.part, self.total = parts, part, total
        rows = total // 4
        blocks = (me ^ jnp.arange(4, dtype=jnp.int32)) * rows
        inner = (blocks[:, None] + jnp.arange(rows, dtype=jnp.int32)[None, :]).reshape(total)
        start, end = bounds[0], bounds[1]
        self.start, self.end = start, end
        self.inner = inner
        index = part * total + inner
        base = jnp.where(index < start, 0, jnp.where(index < end, start, end))
        self.index = index
        self.scalars = jnp.stack([me.astype(jnp.int32), start, end])
        frequency = 10000.0 ** (-jnp.arange(HD // 2, dtype=f32) * 2.0 / HD)
        angles = (index - base).astype(f32)[:, None] * frequency[None, :]
        cosine, sine = jnp.cos(angles), jnp.sin(angles)
        self.cosine = jnp.concatenate([cosine] * 4, axis=1)
        self.sine = jnp.concatenate([-sine, sine] * 2, axis=1)

    def valid(self, rows):
        return (self.index[:rows] < self.end).astype(f32)[:, None]

    def rotate_parts(self, value, shift):
        if shift % self.parts == 0:
            return value
        total = lax.axis_size(("sz", "sy"))
        pairs = []
        for t in range(total):
            head = t - t % self.parts
            pairs.append((head + (t + shift) % self.parts, t))
        return lax.ppermute(value, ("sz", "sy"), pairs)

    def forward(self, part, first):
        total, width = self.total, part.shape[1] // 3
        if self.parts == 1:
            operands = [self.scalars, self.cosine, self.sine, part]
            if first is not None:
                operands.append(first)
            shape = jax.ShapeDtypeStruct((total, width), bf16)
            return kernel_call(
                functools.partial(attention_kernel, first is not None),
                [shape] * 4,
                operands,
                flops=3 * total * total * width,
            )
        query = turn(part[:, :width], self.cosine, self.sine).astype(bf16)
        key = turn(part[:, width : 2 * width], self.cosine, self.sine).astype(bf16)
        value = part[:, 2 * width :]
        if first is not None:
            value = 0.5 * value + 0.5 * first[:, 2 * width :]
        value = value.astype(bf16)
        keys, values = self.slot(key), self.slot(value)

        def one(items):
            q, k, v = items
            return dot(softmax_rows(dot_cols(q, k), self.allowed()).astype(bf16), v)

        out = lax.map(one, (self.heads(query), self.heads(keys), self.heads(values)))
        return (query, key, value, self.rows(out).astype(bf16))

    def slot(self, value):
        return jnp.concatenate([self.rotate_parts(value, r) for r in range(self.parts)])

    def heads(self, rows):
        return rows.reshape(rows.shape[0], -1, HD).transpose(1, 0, 2)

    def rows(self, heads):
        return heads.transpose(1, 0, 2).reshape(heads.shape[1], -1)

    def allowed(self):
        key = jnp.concatenate(
            [(self.part + r) % self.parts * self.total + self.inner for r in range(self.parts)]
        )
        query = self.index[:, None]
        lowest = jnp.where(
            query < self.start, 0, jnp.where(query < self.end, self.start, self.end)
        )
        return (key[None, :] <= query) & (key[None, :] >= lowest)

    def backward(self, saved, up, carry, last):
        query, key, value = saved
        total, width = query.shape
        if self.parts == 1:
            operands = [self.scalars, self.cosine, self.sine, query, key, value, up]
            if last:
                operands.append(carry)
            return kernel_call(
                functools.partial(attention_back_kernel, last),
                [
                    jax.ShapeDtypeStruct((total, 3 * width), bf16),
                    jax.ShapeDtypeStruct((total, width), f32),
                ],
                operands,
                [pltpu.VMEM((total, width), f32)] * 2,
                flops=7 * total * total * width,
            )
        keys, values = self.slot(key), self.slot(value)

        def one(items):
            q, k, v, u = items
            chance = softmax_rows(dot_cols(q, k), self.allowed())
            back = dot_cols(u, v)
            delta = jnp.sum(chance * back, axis=-1, keepdims=True)
            score = (chance * (back - delta) * 0.125).astype(bf16)
            return (dot(score, k), dot_rows(score, q), dot_rows(chance.astype(bf16), u))

        dq, dk, dv = lax.map(
            one, (self.heads(query), self.heads(keys), self.heads(values), self.heads(up))
        )
        dk, dv = self.collect(self.rows(dk)), self.collect(self.rows(dv))
        dv = dv + carry if last else 0.5 * dv
        back_turn = functools.partial(turn, cosine=self.cosine, sine=-self.sine)
        joined = jnp.concatenate([back_turn(self.rows(dq)), back_turn(dk), dv], axis=1)
        return (joined.astype(bf16), dv)

    def collect(self, slot_rows):
        pieces = slot_rows.reshape(self.parts, self.total, -1)
        result = pieces[0]
        for r in range(1, self.parts):
            result = result + self.rotate_parts(pieces[r].astype(bf16), -r).astype(f32)
        return result


def routes(seq_size, group_size, slots_here):
    slots = slots_here * group_size
    parts = seq_size // slots
    result = []
    for r in range(slots_here):
        pairs = []
        for s in range(seq_size):
            for f in range(group_size):
                slot = slots_here * f + (s + r) % slots_here
                t = slot * parts + s // slots
                k = s % slots // slots_here
                pairs.append((s * group_size + f, t * group_size + k))
        result.append(pairs)
    return result


def shards(tokens, doc_bounds, w_qkv, w_out, w_gate, w_up, w_down, norm_attn, norm_mlp, out_grad):
    slots_here, block, model = tokens.shape
    seq_size = lax.axis_size(("sz", "sy"))
    group_size = lax.axis_size(("fx", "fc"))
    sz_size = seq_size // 2
    seq_at = lax.axis_index(("sz", "sy"))
    me = lax.axis_index(("fx", "fc"))
    parts = seq_size // (slots_here * group_size)
    local = slots_here * block
    total = local * group_size
    width = model // group_size
    in_rows = w_qkv.shape[1]
    group_rows = in_rows * group_size
    hidden_rows = w_down.shape[1]
    hidden_here = hidden_rows * seq_size
    paths = routes(seq_size, group_size, slots_here)
    backs = [[(target, source) for source, target in pairs] for pairs in paths]

    def to_group(array):
        got = [
            lax.ppermute(pick(array, (seq_at + r) % 2), ALL, paths[r]) for r in range(slots_here)
        ]
        return in_order(seq_at // parts % 2, got[0], got[1], 0).reshape(local, model)

    def from_group(rows):
        rows = rows.astype(bf16).reshape(slots_here, block, model)
        at = seq_at // parts % 2
        got = [lax.ppermute(pick(rows, (at + r) % 2), ALL, backs[r]) for r in range(slots_here)]
        return in_order(seq_at % 2, got[0], got[1], 0).astype(f32)

    bounds = lax.ppermute(pick(doc_bounds, seq_at % 2), ALL, paths[0])
    hidden = to_group(tokens).astype(f32)
    attention = Attention(me, seq_at % parts, parts, total, bounds)
    valid = attention.valid(local)

    gains = jnp.stack([norm_attn[0], norm_mlp[0], norm_attn[1], norm_mlp[1]], axis=1)
    gains = jnp.pad(gains, ((0, 0), (0, 124)))

    def gathered(own):
        return lax.all_gather(own, "sz", axis=0, tiled=False)

    def attention_weights(layer):
        pieces = w_qkv[layer].reshape(in_rows, 3, group_size, width).transpose(2, 0, 1, 3)
        pieces = pieces.reshape(group_size, in_rows, 3 * width)
        if layer == 0:
            extra = jnp.broadcast_to(gains[None], (group_size, in_rows, 128))
            pieces = jnp.concatenate([pieces, extra], axis=2)
        mine = exchange(pieces).reshape(group_rows, -1)
        outs = w_out[layer].reshape(in_rows, group_size, width).transpose(1, 0, 2)
        own = gathered(jnp.concatenate([mine, outs.reshape(group_rows, width)], axis=1))
        wide = mine.shape[1]
        into = join_y(own[:, :, :wide])
        outs = own[:, :, wide:].reshape(group_size, -1, group_size, in_rows, width)
        outs = exchange(outs.transpose(0, 1, 3, 2, 4).reshape(group_size, -1, in_rows, model))
        outs = in_order(lax.axis_index("sy"), outs, swap_y(outs), 0)
        outs = outs.transpose(2, 0, 1, 3, 4).reshape(width, model)
        return (into, outs)

    def mlp_weights(layer):
        def cut(weight):
            weight = weight[layer].reshape(in_rows, seq_size, group_size, hidden_rows)
            return weight.transpose(2, 0, 1, 3).reshape(group_size, in_rows, hidden_here)

        mine = exchange(jnp.stack([cut(w_gate), cut(w_up)], axis=1))
        mine = mine.transpose(1, 0, 2, 3).reshape(2 * group_rows, hidden_here)
        own = gathered(mine)
        return (join_y(own[:, :group_rows]), join_y(own[:, group_rows:]))

    weights = []
    in_first, out_first = attention_weights(0)
    gain_rows = in_first[:, 3 * width : 3 * width + 4].astype(f32).T
    weights.append((in_first[:, : 3 * width], out_first) + mlp_weights(0))
    downs = gathered(jnp.concatenate([w_down[0], w_down[1]]))
    downs = [join_y(downs[:, :hidden_rows]), join_y(downs[:, hidden_rows:])]
    weights.append(attention_weights(1) + mlp_weights(1))

    saved = []
    first = None
    for layer in range(LAYERS):
        qkv_w, out_w, gate_w, up_w = weights[layer]
        normed_attn, inverse_attn = normalize(hidden)
        attn_in = spread((normed_attn * gain_rows[2 * layer]).astype(bf16))
        part = jnp.concatenate([dot(rows, qkv_w) for rows in attn_in])
        query, key, value, out = attention.forward(part, first)
        if first is None:
            first = part
        outs = (out[: total // 2], out[total // 2 :])
        middle = hidden + gather_sum(dot(outs[0], out_w), dot(outs[1], out_w))
        normed_mlp, inverse_mlp = normalize(middle)
        mlp_in = spread((normed_mlp * gain_rows[2 * layer + 1]).astype(bf16))
        gates = [dot(rows, gate_w) for rows in mlp_in]
        ups = [dot(rows, up_w) for rows in mlp_in]
        active = [(jax.nn.silu(g) * u).astype(bf16) for g, u in zip(gates, ups)]
        hidden = middle + gather_sum(dot(active[0], downs[layer]), dot(active[1], downs[layer]))
        saved.append(
            (normed_attn, inverse_attn, attn_in, (query, key, value), outs)
            + (normed_mlp, inverse_mlp, mlp_in, gates, ups, active)
        )
    hidden_out = from_group(hidden * valid)

    upstream = to_group(out_grad).astype(f32) * valid
    carry = None
    grads = [None] * LAYERS
    for layer in reversed(range(LAYERS)):
        qkv_w, out_w, gate_w, up_w = weights[layer]
        (normed_attn, inverse_attn, attn_in, attn_saved, outs) = saved[layer][:5]
        (normed_mlp, inverse_mlp, mlp_in, gates, ups, active) = saved[layer][5:]
        mlp_up = spread(upstream.astype(bf16))
        gate_grads, up_grads = [], []
        for rows, gate, up in zip(mlp_up, gates, ups):
            act_grad = dot_cols(rows, downs[layer])
            sigmoid = jax.nn.sigmoid(gate)
            gate_grads.append(
                (act_grad * up * sigmoid * (1.0 + gate * (1.0 - sigmoid))).astype(bf16)
            )
            up_grads.append((act_grad * (gate * sigmoid)).astype(bf16))
        mlp_in_grad = gather_sum(
            *[dot_cols(g, gate_w) + dot_cols(u, up_w) for g, u in zip(gate_grads, up_grads)]
        )

        def sum_dots(lefts, rights):
            return (dot_rows(lefts[0], rights[0]) + dot_rows(lefts[1], rights[1])).astype(bf16)

        grad_down = reduce_rows(sum_dots(active, mlp_up), hidden_rows)
        grad_gate = sum_dots(mlp_in, gate_grads).reshape(sz_size, 2, group_rows, hidden_here)
        grad_up = sum_dots(mlp_in, up_grads).reshape(sz_size, 2, group_rows, hidden_here)
        pair = reduce_rows(jnp.concatenate([grad_gate, grad_up], axis=2), 2 * group_rows)
        pair = pair.reshape(2, group_size, in_rows, hidden_here).transpose(1, 0, 2, 3)
        pair = exchange(pair).reshape(group_size, 2, in_rows, seq_size, hidden_rows)
        pair = pair.transpose(1, 2, 3, 0, 4).reshape(2, in_rows, -1)

        norm_part, mlp_gain = norm_back(
            mlp_in_grad, normed_mlp, inverse_mlp, gain_rows[2 * layer + 1]
        )
        upstream = upstream + norm_part
        attn_up = spread(upstream.astype(bf16))
        out_back = jnp.concatenate([dot_cols(rows, out_w).astype(bf16) for rows in attn_up])
        joined, value_grad = attention.backward(attn_saved, out_back, carry, layer == 0)
        if layer > 0:
            carry = value_grad if carry is None else carry + value_grad
        halves = (joined[: total // 2], joined[total // 2 :])
        attn_in_grad = gather_sum(*[dot_cols(rows, qkv_w) for rows in halves])
        norm_part, attn_gain = norm_back(
            attn_in_grad, normed_attn, inverse_attn, gain_rows[2 * layer]
        )
        upstream = upstream + norm_part

        grad_qkv = sum_dots(attn_in, halves)
        extra = jnp.stack([attn_gain, mlp_gain], axis=1).astype(bf16)
        grad_qkv = jnp.concatenate([grad_qkv, jnp.pad(extra, ((0, 0), (0, 126)))], axis=1)
        grad_outw = sum_dots(outs, attn_up).reshape(-1, 2, group_size, in_rows, model)
        grad_outw = exchange(grad_outw.transpose(2, 0, 1, 3, 4))
        grad_outw = grad_outw.reshape(seq_size, in_rows, group_size, width)
        grad_outw = grad_outw.transpose(0, 2, 1, 3).reshape(model, width)
        mixed = reduce_rows(jnp.concatenate([grad_qkv, grad_outw], axis=1), group_rows)
        wide = grad_qkv.shape[1]
        outw = mixed[:, wide:].reshape(group_size, in_rows, width)
        outw = outw.transpose(1, 0, 2).reshape(in_rows, model)
        mixed = exchange(mixed[:, :wide].reshape(group_size, in_rows, wide)).astype(f32)
        gain_sums = jnp.sum(mixed[:, :, 3 * width : 3 * width + 2], axis=0)
        qkv = mixed[:, :, : 3 * width].reshape(group_size, in_rows, 3, width)
        qkv = qkv.transpose(1, 2, 0, 3).reshape(in_rows, 3 * model)
        grads[layer] = (qkv, outw, pair[0], pair[1], grad_down, gain_sums[:, 0], gain_sums[:, 1])

    pieces = value_grad.astype(bf16).reshape(group_size, local, width)
    order = me ^ jnp.arange(group_size, dtype=jnp.int32)
    pieces = jnp.take(pieces, order, axis=0)
    first_grad = exchange(pieces).transpose(1, 0, 2).reshape(local, model)
    stacked = [
        jnp.stack([grads[layer][member].astype(f32) for layer in range(LAYERS)])
        for member in range(7)
    ]
    return (hidden_out, from_group(upstream), *stacked, from_group(first_grad))


def solution(mesh):
    seq, fsdp = mesh.shape["seq"], mesh.shape["fsdp"]
    inner = Mesh(mesh.devices.reshape(seq // 2, 2, fsdp // 2, 2), ALL)
    rows = P(("fx", "fc"), ("sz", "sy"), None)
    weight, gain = P(None, ALL, None), P(None, ALL)
    in_specs = (rows, P(("fx", "fc"), None)) + (weight,) * 5 + (gain,) * 2 + (rows,)
    out_specs = (rows, rows) + (weight,) * 5 + (gain,) * 2 + (rows,)
    return jax.shard_map(
        shards, mesh=inner, in_specs=in_specs, out_specs=out_specs, check_vma=False
    )
```

```python
import functools

import jax
import jax.numpy as jnp
from jax import lax
from jax.experimental import pallas as pl
from jax.experimental.pallas import tpu as pltpu
from jax.sharding import Mesh, PartitionSpec as P

HD = 64
LAYERS = 2
epsilon = 1e-05
masked_score = -1e30
bf16 = jnp.bfloat16
f32 = jnp.float32

ALL = ("sz", "sy", "fx", "fc")
SWAP = ((0, 1), (1, 0))
VMEM_LIMIT = 24 * 1024 * 1024


def dot(left, right):
    return jnp.dot(left, right, preferred_element_type=f32)


def dot_rows(left, right):
    return lax.dot_general(left, right, (((0,), (0,)), ((), ())), preferred_element_type=f32)


def dot_cols(left, right):
    return lax.dot_general(left, right, (((1,), (1,)), ((), ())), preferred_element_type=f32)


def swap_core(value):
    return lax.ppermute(value, "fc", SWAP)


def swap_x(value):
    return lax.ppermute(value, "fx", SWAP)


def swap_y(value):
    return lax.ppermute(value, "sy", SWAP)


def pick(array, index, axis=0):
    return lax.dynamic_index_in_dim(array, index, axis, keepdims=False)


def in_order(flag, first, second, axis):
    return jnp.where(
        flag == 0, jnp.stack([first, second], axis), jnp.stack([second, first], axis)
    )


def exchange(pieces):
    fx, fc = lax.axis_index("fx"), lax.axis_index("fc")
    pieces = pieces.reshape((2, 2) + pieces.shape[1:])
    got = swap_x(pick(pieces, 1 - fx))
    both = in_order(fx, pick(pieces, fx), got, 0)
    got = swap_core(pick(both, 1 - fc, 1))
    both = in_order(fc, pick(both, fc, 1), got, 1)
    return both.reshape((4,) + both.shape[2:])


def sum_near(value):
    value = value + swap_x(value)
    value = value + swap_core(value)
    half = value.shape[1] // 2
    got = swap_y(value)
    return value[:, :half] + got[:, half:]


def steps_z():
    size = lax.axis_size("sz")
    return [(d, [(i, i ^ d) for i in range(size)]) for d in range(1, size)]


def gather_near(block):
    return [block] + [lax.ppermute(block, "sz", pairs) for _, pairs in steps_z()]


def scatter_near(blocks):
    total = blocks[0].astype(f32)
    for d, pairs in steps_z():
        total = total + lax.ppermute(blocks[d], "sz", pairs).astype(f32)
    return total


def by_distance(rows):
    at = lax.axis_index("sz")
    return [pick(rows, at ^ d) for d in range(rows.shape[0])]


def scattered(total):
    return lax.psum_scatter(total, "sz", scatter_dimension=0, tiled=False)


def spread(value):
    over = swap_x(value)
    return (value, swap_core(value), over, swap_core(over))


def kernel_call(body, results, scalars, operands, scratch, after, flops):
    count, extra = len(operands), len(after)

    def whole(scalars_ref, *refs):
        body(scalars_ref, *refs[:count], *refs[count + extra :])

    vmem = pl.BlockSpec(memory_space=pltpu.VMEM)
    return pl.pallas_call(
        whole,
        out_shape=[shape_of(*one) for one in results],
        in_specs=[pl.BlockSpec(memory_space=pltpu.SMEM)]
        + [vmem] * count
        + [pl.BlockSpec(memory_space=pl.ANY)] * extra,
        out_specs=[vmem] * len(results),
        scratch_shapes=list(scratch),
        compiler_params=pltpu.CompilerParams(vmem_limit_bytes=VMEM_LIMIT),
        cost_estimate=pl.CostEstimate(
            flops=1, bytes_accessed=1, transcendentals=0
        ),
    )(scalars, *operands, *after)


def shape_of(shape, dtype):
    return jax.ShapeDtypeStruct(shape, dtype)


def block_pairs(scalars, width):
    half, me_y = width // 256, scalars[3]
    for i in range(half):
        yield (i * 128, pl.multiple_of((2 * i + me_y) * 128, 128))
        yield ((half + i) * 128, pl.multiple_of((2 * i + 1 - me_y) * 128, 128))


def norm_kernel(added, scalars, *refs):
    inputs, (gain_ref, sum_ref, out_ref) = refs[:added], refs[added:]
    total = inputs[0][...].astype(f32)
    for ref in inputs[1:]:
        total += (ref[...] if len(ref.shape) == 2 else ref[0]).astype(f32)
    sum_ref[...] = total
    inverse = lax.rsqrt(jnp.mean(total * total, axis=-1, keepdims=True) + epsilon)
    for local, natural in block_pairs(scalars, sum_ref.shape[1]):
        normed = sum_ref[:, pl.ds(natural, 128)] * inverse
        out_ref[:, local : local + 128] = (normed * gain_ref[:, local : local + 128]).astype(bf16)


def norm_back_kernel(scalars, up_ref, d0, d1, d2, z_ref, gain_ref, up_out, low_out, gain_out, work):
    z = z_ref[...]
    inverse = lax.rsqrt(jnp.mean(z * z, axis=-1, keepdims=True) + epsilon)
    for local, natural in block_pairs(scalars, z.shape[1]):
        here = slice(local, local + 128)
        core = d1[:, here] if len(d1.shape) == 2 else d1[0, :, here]
        dy = d0[:, here] + core.astype(f32) + d2[:, here].astype(f32)
        normed = z_ref[:, pl.ds(natural, 128)] * inverse
        gain_out[:, here] = jnp.sum(dy * normed, axis=0, keepdims=True)
        work[:, pl.ds(natural, 128)] = dy * gain_ref[:, here]
    scaled = work[...]
    normed = z * inverse
    mean = jnp.mean(scaled * normed, axis=-1, keepdims=True)
    up = up_ref[...] + inverse * (scaled - normed * mean)
    up_out[...] = up
    low_out[...] = up.astype(bf16)


def add_kernel(scalars, left, right, out_ref):
    out_ref[...] = (left[...].astype(f32) + right[...].astype(f32)).astype(out_ref.dtype)


def add_second_kernel(scalars, left, right, out_ref):
    out_ref[...] = (left[...] + right[1].astype(f32)).astype(out_ref.dtype)


def add_pair_kernel(scalars, left, right, second_left, second_right, out_ref):
    size = left.shape[2]
    out_ref[:, :, :size] = (left[...].astype(f32) + right[...].astype(f32)).astype(bf16)
    out_ref[:, :, size:] = (second_left[...].astype(f32) + second_right[...].astype(f32)).astype(bf16)


def hold_kernel(scalars, value, out_ref):
    out_ref[...] = value[...]


def partner(rows):
    lane = lax.broadcasted_iota(jnp.int32, rows.shape, 1)
    return jnp.where(lane % 64 < 32, pltpu.roll(rows, 96, 1), pltpu.roll(rows, 32, 1))


def block_mask(block, rows, start, end):
    shape = (rows, (block + 1) * rows)
    query = block * rows + lax.broadcasted_iota(jnp.int32, (rows, 1), 0)
    lowest = jnp.where(query < start, 0, jnp.where(query < end, start, end))
    key = lax.broadcasted_iota(jnp.int32, shape, 1)
    return (key <= query) & (key >= lowest)


def softmax_rows(scores, allowed):
    scores = jnp.where(allowed, scores * 0.125, masked_score)
    weights = jnp.exp(scores - jnp.max(scores, axis=-1, keepdims=True))
    return weights * (1.0 / jnp.sum(weights, axis=-1, keepdims=True))


def flat(ref, first, last):
    value = ref[:, first:last, :]
    return value.reshape(-1, value.shape[-1])


def rows_of(refs, columns):
    values = []
    for ref in refs:
        if len(ref.shape) == 3:
            values.append(ref[:, :, :columns].reshape(-1, columns))
        else:
            values.append(ref[:, :columns])
    return values[0] if len(values) == 1 else jnp.concatenate(values, axis=0)


def place(ref, me_y, own, other):
    half = own.shape[0]
    ref[pl.ds(pl.multiple_of(me_y * half, half), half), :] = own
    ref[pl.ds(pl.multiple_of((1 - me_y) * half, half), half), :] = other


def attention_kernel(blend, count, scalars, a0, a1, a2, a3, *refs):
    own, other, refs = refs[:count], refs[count : 2 * count], refs[2 * count :]
    cos_ref, sin_ref, refs = refs[0], refs[1], refs[2:]
    if blend:
        first_ref, q_ref, k_ref, v_ref, o_ref = refs
    else:
        q_ref, k_ref, v_ref, o_ref, first_ref = refs
    me, start, end = scalars[0], scalars[1], scalars[2]
    total, width = q_ref.shape
    rows = total // 4
    here_w, there_w = rows_of(own, 3 * width), rows_of(other, 3 * width)
    half = here_w.shape[0]
    for i, a_ref in enumerate((a0, a1, a2, a3)):
        part = dot(a_ref[:, :half], here_w) + dot(a_ref[:, half:], there_w)
        here = slice(i * rows, (i + 1) * rows)
        there = pl.ds(pl.multiple_of((me ^ i) * rows, rows), rows)
        cosine, sine = cos_ref[here, :], sin_ref[here, :]
        for j in range(width // 128):
            for into, at in ((q_ref, 0), (k_ref, width)):
                piece = part[:, at + j * 128 : at + (j + 1) * 128]
                turned = piece * cosine + partner(piece) * sine
                into[there, j * 128 : (j + 1) * 128] = turned.astype(bf16)
        value = part[:, 2 * width :]
        if blend:
            value = 0.5 * value + 0.5 * first_ref[there, :]
        else:
            first_ref[there, :] = value
        v_ref[there, :] = value.astype(bf16)
    lane = lax.broadcasted_iota(jnp.int32, (rows, 128), 1)
    for b in range(4):
        allowed = block_mask(b, rows, start, end)
        there = pl.ds(pl.multiple_of((me ^ b) * rows, rows), rows)
        for j in range(width // 128):
            columns = slice(j * 128, (j + 1) * 128)
            query = q_ref[b * rows : (b + 1) * rows, columns]
            keys = k_ref[: (b + 1) * rows, columns]
            values = v_ref[: (b + 1) * rows, columns]
            outs = []
            for h in range(2):
                one = jnp.where(lane // 64 == h, query, jnp.zeros_like(query))
                chance = softmax_rows(dot_cols(one, keys), allowed)
                outs.append(dot(chance.astype(bf16), values))
            o_ref[there, columns] = jnp.where(lane < 64, outs[0], outs[1]).astype(bf16)


def out_kernel(scalars, o_ref, out_w, near, far, cores):
    rows = near.shape[0]
    cores[1] = dot(o_ref[3 * rows :, :], out_w[...]).astype(bf16)
    cores[0] = dot(o_ref[rows : 2 * rows, :], out_w[...]).astype(bf16)
    far[...] = dot(o_ref[2 * rows : 3 * rows, :], out_w[...])
    near[...] = dot(o_ref[:rows, :], out_w[...])


def attention_back_kernel(last, count, scalars, y0, y1, y2, y3, *refs):
    own, other, refs = refs[:count], refs[count : 2 * count], refs[2 * count :]
    out_w, cos_ref, sin_ref, q_ref, k_ref, v_ref = refs[:6]
    refs = refs[6:]
    if last:
        carry_ref, near, far, cores, d_ref, dv_ref, dk_sum, dv_sum, up_ref = refs
    else:
        near, far, cores, d_ref, dv_ref, dk_sum, dv_sum, up_ref = refs
    me, start, end = scalars[0], scalars[1], scalars[2]
    total, width = q_ref.shape
    rows = total // 4
    for i, y_ref in enumerate((y0, y1, y2, y3)):
        there = pl.ds(pl.multiple_of((me ^ i) * rows, rows), rows)
        up_ref[there, :] = dot_cols(y_ref[...], out_w[...]).astype(bf16)
    lane = lax.broadcasted_iota(jnp.int32, (rows, 128), 1)
    dk_sum[...] = jnp.zeros_like(dk_sum)
    dv_sum[...] = jnp.zeros_like(dv_sum)
    for b in range(4):
        allowed = block_mask(b, rows, start, end)
        there = pl.ds(pl.multiple_of((me ^ b) * rows, rows), rows)
        upto = slice(0, (b + 1) * rows)
        cosine, sine = cos_ref[there, :], sin_ref[there, :]
        for j in range(width // 128):
            columns = slice(j * 128, (j + 1) * 128)
            query = q_ref[b * rows : (b + 1) * rows, columns]
            keys, values = k_ref[upto, columns], v_ref[upto, columns]
            up = up_ref[b * rows : (b + 1) * rows, columns]
            dq, dk, dv = [], [], []
            for h in range(2):
                mine = lane // 64 == h
                one = jnp.where(mine, query, jnp.zeros_like(query))
                one_up = jnp.where(mine, up, jnp.zeros_like(up))
                chance = softmax_rows(dot_cols(one, keys), allowed)
                back = dot_cols(one_up, values)
                delta = jnp.sum(chance * back, axis=-1, keepdims=True)
                score = (chance * (back - delta) * 0.125).astype(bf16)
                dq.append(dot(score, keys))
                dk.append(dot_rows(score, one))
                dv.append(dot_rows(chance.astype(bf16), one_up))
            dk_sum[upto, columns] += dk[0] + dk[1]
            dv_sum[upto, columns] += dv[0] + dv[1]
            dq = jnp.where(lane < 64, dq[0], dq[1])
            d_ref[there, columns] = (dq * cosine - partner(dq) * sine).astype(bf16)
    for b in range(4):
        there = pl.ds(pl.multiple_of((me ^ b) * rows, rows), rows)
        here = slice(b * rows, (b + 1) * rows)
        cosine, sine = cos_ref[there, :], sin_ref[there, :]
        for j in range(width // 128):
            dk = dk_sum[here, j * 128 : (j + 1) * 128]
            dk = dk * cosine - partner(dk) * sine
            d_ref[there, width + j * 128 : width + (j + 1) * 128] = dk.astype(bf16)
        dv = dv_sum[here, :]
        dv = dv + carry_ref[here, :] if last else 0.5 * dv
        dv_ref[here, :] = dv
        d_ref[there, 2 * width : 3 * width] = dv.astype(bf16)
    here_w, there_w = rows_of(own, 3 * width), rows_of(other, 3 * width)
    half = here_w.shape[0]
    for at, weight in ((slice(0, half), here_w), (slice(half, 2 * half), there_w)):
        for i in range(4):
            total_d = dot_cols(d_ref[i * rows : (i + 1) * rows, :], weight)
            if i % 2:
                cores[i // 2, :, at] = total_d.astype(bf16)
            else:
                (far if i else near)[:, at] = total_d


def mlp_halves(ref):
    size = ref.shape[2] // 2
    blocks = range(ref.shape[0])
    return [
        jnp.concatenate([ref[z, :, at : at + size] for z in blocks], axis=1) for at in (0, size)
    ]


def mlp_kernel(scalars, m0, m1, own, other, down_own, down_other, p0, p1, g_ref, u_ref, z_ref, down):
    rows = m0.shape[0]
    place(down, scalars[3], down_own[...], down_other[...])
    gate_own, up_own = mlp_halves(own)
    gate_other, up_other = mlp_halves(other)
    half = gate_own.shape[1]
    for i, (m_ref, p_ref) in enumerate(((m0, p0), (m1, p1))):
        here = slice(i * rows, (i + 1) * rows)
        left, right = m_ref[:, :half], m_ref[:, half:]
        gate = dot_cols(left, gate_own) + dot_cols(right, gate_other)
        up = dot_cols(left, up_own) + dot_cols(right, up_other)
        active = (jax.nn.silu(gate) * up).astype(bf16)
        g_ref[here, :] = gate.astype(bf16)
        u_ref[here, :] = up.astype(bf16)
        z_ref[here, :] = active
        p_ref[...] = dot(active, down[...]).astype(p_ref.dtype)


def mlp_back_kernel(scalars, y0, y1, g_ref, u_ref, own, other, down_own, down_other, p0, p1, dg_ref, du_ref, down):
    rows = y0.shape[0]
    place(down, scalars[3], down_own[...], down_other[...])
    gate_own, up_own = mlp_halves(own)
    gate_other, up_other = mlp_halves(other)
    half = gate_own.shape[1]
    for i, (y_ref, p_ref) in enumerate(((y0, p0), (y1, p1))):
        here = slice(i * rows, (i + 1) * rows)
        back = dot_cols(y_ref[...], down[...])
        gate, up = g_ref[here, :].astype(f32), u_ref[here, :].astype(f32)
        sigmoid = jax.nn.sigmoid(gate)
        dg = (back * up * sigmoid * (1.0 + gate * (1.0 - sigmoid))).astype(bf16)
        du = (back * (gate * sigmoid)).astype(bf16)
        dg_ref[here, :] = dg
        du_ref[here, :] = du
        p_ref[:, :half] = (dot(dg, gate_own) + dot(du, up_own)).astype(p_ref.dtype)
        p_ref[:, half:] = (dot(dg, gate_other) + dot(du, up_other)).astype(p_ref.dtype)


def gate_grad_kernel(scalars, m0, m1, m2, m3, near, far, keep, send):
    rows = m0.shape[0]
    blocks, size = keep.shape[0], keep.shape[2]
    half = blocks * size
    for into, columns in ((send, slice(half, 2 * half)), (keep, slice(0, half))):
        total = dot_rows(near[:rows, :], m0[:, columns])
        total += dot_rows(near[rows:, :], m1[:, columns])
        total += dot_rows(far[:rows, :], m2[:, columns])
        total += dot_rows(far[rows:, :], m3[:, columns])
        for z in range(blocks):
            into[z] = total[:, z * size : (z + 1) * size].astype(bf16)


def rows_grad_kernel(scalars, left_near, left_far, y0, y1, y2, y3, keep, send, work):
    rows = y0.shape[0]
    half = keep.shape[0]
    work[...] = dot_rows(left_near[:rows, :], y0[...]) + dot_rows(left_near[rows:, :], y1[...])
    work[...] += dot_rows(left_far[:rows, :], y2[...]) + dot_rows(left_far[rows:, :], y3[...])
    me_y = scalars[3]
    keep[...] = work[pl.ds(pl.multiple_of(me_y * half, half), half), :].astype(bf16)
    send[...] = work[pl.ds(pl.multiple_of((1 - me_y) * half, half), half), :].astype(bf16)


def qkv_grad_kernel(scalars, a0, a1, a2, a3, d_ref, keep, send):
    rows = a0.shape[0]
    blocks, size = keep.shape[0], keep.shape[1]
    half = blocks * size
    for into, columns in ((send, slice(half, 2 * half)), (keep, slice(0, half))):
        total = dot_rows(a0[:, columns], d_ref[:rows, :])
        for i, a_ref in ((1, a1), (2, a2), (3, a3)):
            total += dot_rows(a_ref[:, columns], d_ref[i * rows : (i + 1) * rows, :])
        into[...] = total.astype(bf16).reshape(blocks, size, -1)


def turn(rows, cosine, sine):
    total, width = rows.shape
    halves = rows.reshape(total, width // HD, 2, HD // 2)
    cosine = cosine[:, :HD].reshape(total, 1, 2, HD // 2)
    sine = sine[:, :HD].reshape(total, 1, 2, HD // 2)
    return (halves * cosine + halves[:, :, ::-1] * sine).reshape(total, width)


class Group:
    def __init__(self, local, model, width, parts, bounds):
        self.local, self.model, self.width, self.parts = local, model, width, parts
        self.total = total = 4 * local
        self.me_y = lax.axis_index("sy")
        self.blocks = lax.axis_size("sz")
        me = lax.axis_index(("fx", "fc"))
        self.part = lax.axis_index(("sz", "sy")) % parts
        order = (me ^ jnp.arange(4, dtype=jnp.int32)) * local
        self.inner = (order[:, None] + jnp.arange(local, dtype=jnp.int32)[None, :]).reshape(total)
        self.start, self.end = bounds[0], bounds[1]
        self.index = index = self.part * total + self.inner
        self.me_z = lax.axis_index("sz")
        self.scalars = jnp.stack([me, self.start, self.end, self.me_y, self.me_z]).astype(jnp.int32)
        base = jnp.where(index < self.start, 0, jnp.where(index < self.end, self.start, self.end))
        frequency = 10000.0 ** (-jnp.arange(HD // 2, dtype=f32) * 2.0 / HD)
        angles = (index - base).astype(f32)[:, None] * frequency[None, :]
        cosine, sine = jnp.cos(angles), jnp.sin(angles)
        self.cosine = jnp.concatenate([cosine] * 4, axis=1)
        self.sine = jnp.concatenate([-sine, sine] * 2, axis=1)
        self.block = model // (2 * self.blocks)
        self.latest, self.needed = None, []

    def call(self, body, shapes, operands, scratch=(), micros=1):
        after = self.needed + ([] if self.latest is None else [self.latest])
        self.needed = []
        flops = int(micros * 1e9)
        got = kernel_call(body, shapes, self.scalars, operands, scratch, after, flops)
        self.latest = got[-1]
        return got

    def add(self, left, right):
        return self.call(add_kernel, [(left.shape, bf16)], [left, right])[0]

    def need(self, *values):
        self.needed += values

    def add_pair(self, first, second):
        shape = (*first[0].shape[:2], 2 * first[0].shape[2])
        if self.block % 128:
            sums = [self.add(*one) for one in (first, second)]
            return jnp.concatenate(sums, axis=2)
        return self.call(add_pair_kernel, [(shape, bf16)], [*first, *second])[0]

    def hold(self, value):
        return self.call(hold_kernel, [(value.shape, value.dtype)], [value])[0]

    def reduce_pieces(self, pieces):
        if len(pieces) == 3:
            got = swap_core(pieces[2])
            out = self.call(
                add_second_kernel,
                [(pieces[1].shape, bf16)],
                [pieces[1], got],
            )[0]
            return (pieces[0], got, swap_x(out))
        got = swap_core(pieces[3])
        out = self.call(
            add_kernel, [(got.shape, bf16)], [pieces[2], got]
        )[0]
        return (pieces[0], swap_core(pieces[1]), swap_x(out))

    def sum_y(self, keep, send):
        return self.add(keep, send)

    def valid(self):
        return (self.index[: self.local] < self.end).astype(f32)[:, None]

    def to_local(self, rows):
        cut = rows.reshape(rows.shape[0], self.blocks, 2, self.block)
        pair = in_order(self.me_y, cut[:, :, 0], cut[:, :, 1], 1)
        return pair.reshape(rows.shape[0], self.model)

    def to_natural(self, rows):
        cut = rows.reshape(rows.shape[0], 2, self.blocks, self.block)
        cut = in_order(self.me_y, cut[:, 0], cut[:, 1], 2)
        return cut.reshape(rows.shape[0], self.model)

    def plain_sum(self, pieces):
        return sum((one if one.ndim == 2 else one[0]).astype(f32) for one in pieces)

    def norm(self, pieces, gain):
        if self.block % 128 == 0:
            shape = (self.local, self.model)
            return self.call(
                functools.partial(norm_kernel, len(pieces)),
                [(shape, f32), (shape, bf16)],
                [*pieces, gain],
            )
        total = self.plain_sum(pieces)
        inverse = lax.rsqrt(jnp.mean(total * total, axis=-1, keepdims=True) + epsilon)
        return (total, (self.to_local(total * inverse) * gain).astype(bf16))

    def norm_back(self, up, pieces, z, gain):
        if self.block % 128 == 0:
            shape = (self.local, self.model)
            return self.call(
                norm_back_kernel,
                [(shape, f32), (shape, bf16), ((1, self.model), f32)],
                [up, *pieces, z, gain],
                [pltpu.VMEM(shape, f32)],
            )
        dy = self.plain_sum(pieces)
        inverse = lax.rsqrt(jnp.mean(z * z, axis=-1, keepdims=True) + epsilon)
        normed = z * inverse
        gain_grad = jnp.sum(dy * self.to_local(normed), axis=0, keepdims=True)
        scaled = self.to_natural(dy * gain)
        mean = jnp.mean(scaled * normed, axis=-1, keepdims=True)
        up = up + inverse * (scaled - normed * mean)
        return (up, up.astype(bf16), gain_grad)

    def pieces(self):
        shape = (self.local, self.model)
        return [(shape, f32), (shape, f32), ((2, *shape), bf16)]

    def cut(self, rows):
        cut = rows.reshape(4, self.local, -1)
        return (cut[0], cut[2], cut[1::2].astype(bf16))

    def attend(self, a, weights, first):
        total, width = self.total, self.width
        tables = [self.cosine, self.sine]
        own, other, out_w = weights
        if self.parts == 1:
            results = [((total, width), bf16)] * 4
            operands = [*a, *own, *other, *tables]
            if first is None:
                results += [((total, width), f32)]
            else:
                operands += [first]
            got = self.call(
                functools.partial(attention_kernel, first is not None, len(own)),
                results,
                operands,
                micros=12,
            )
            partial = self.call(out_kernel, self.pieces(), [got[3], out_w], micros=3)
            return (partial, got[:3], got[3], got[4] if first is None else first)
        own, other = self.plain(own), self.plain(other)
        rows = jnp.concatenate(a)
        part = dot(rows[:, : own.shape[0]], own) + dot(rows[:, own.shape[0] :], other)
        query = turn(part[:, :width], *tables).astype(bf16)
        key = turn(part[:, width : 2 * width], *tables).astype(bf16)
        value = part[:, 2 * width :]
        if first is None:
            first = value
        else:
            value = 0.5 * value + 0.5 * first
        value = value.astype(bf16)

        def one(items):
            q, k, v = items
            return dot(softmax_rows(dot_cols(q, k), self.allowed()).astype(bf16), v)

        packed = (self.heads(query), self.heads(self.slot(key)), self.heads(self.slot(value)))
        out = self.rows(lax.map(one, packed)).astype(bf16)
        return (self.cut(dot(out, out_w)), (query, key, value), out, first)

    def attend_back(self, y, weights, saved, carry, last):
        total, width = self.total, self.width
        own, other, out_w = weights
        if self.parts == 1:
            operands = [*y, *own, *other, out_w, self.cosine, self.sine, *saved]
            if last:
                operands += [carry]
            got = self.call(
                functools.partial(attention_back_kernel, last, len(own)),
                self.pieces() + [((total, 3 * width), bf16), ((total, width), f32)],
                operands,
                [pltpu.VMEM((total, width), f32)] * 2 + [pltpu.VMEM((total, width), bf16)],
                micros=20,
            )
            return (got[:3], got[3], got[4])
        own, other = self.plain(own), self.plain(other)
        query, key, value = saved
        up = dot_cols(jnp.concatenate(y), out_w).astype(bf16)

        def one(items):
            q, k, v, u = items
            chance = softmax_rows(dot_cols(q, k), self.allowed())
            back = dot_cols(u, v)
            delta = jnp.sum(chance * back, axis=-1, keepdims=True)
            score = (chance * (back - delta) * 0.125).astype(bf16)
            return (dot(score, k), dot_rows(score, q), dot_rows(chance.astype(bf16), u))

        packed = (query, self.slot(key), self.slot(value), up)
        dq, dk, dv = lax.map(one, tuple(self.heads(rows) for rows in packed))
        dk, dv = self.collect(self.rows(dk)), self.collect(self.rows(dv))
        dv = dv + carry if last else 0.5 * dv
        back_turn = functools.partial(turn, cosine=self.cosine, sine=-self.sine)
        joined = jnp.concatenate([back_turn(self.rows(dq)), back_turn(dk), dv], axis=1)
        joined = joined.astype(bf16)
        sums = jnp.concatenate([dot_cols(joined, own), dot_cols(joined, other)], axis=1)
        return (self.cut(sums), joined, dv)

    def plain(self, blocks):
        wide = 3 * self.width
        return jnp.concatenate([block[..., :wide].reshape(-1, wide) for block in blocks])

    def rotate_parts(self, value, shift):
        if shift % self.parts == 0:
            return value
        pairs = []
        for t in range(lax.axis_size(("sz", "sy"))):
            head = t - t % self.parts
            pairs.append((head + (t + shift) % self.parts, t))
        return lax.ppermute(value, ("sz", "sy"), pairs)

    def slot(self, value):
        return jnp.concatenate([self.rotate_parts(value, r) for r in range(self.parts)])

    def heads(self, rows):
        return rows.reshape(rows.shape[0], -1, HD).transpose(1, 0, 2)

    def rows(self, heads):
        return heads.transpose(1, 0, 2).reshape(heads.shape[1], -1)

    def allowed(self):
        key = jnp.concatenate(
            [(self.part + r) % self.parts * self.total + self.inner for r in range(self.parts)]
        )
        query = self.index[:, None]
        lowest = jnp.where(
            query < self.start, 0, jnp.where(query < self.end, self.start, self.end)
        )
        return (key[None, :] <= query) & (key[None, :] >= lowest)

    def collect(self, slot_rows):
        pieces = slot_rows.reshape(self.parts, self.total, -1)
        result = pieces[0]
        for r in range(1, self.parts):
            result = result + self.rotate_parts(pieces[r].astype(bf16), -r).astype(f32)
        return result

    def mlp(self, m, weights):
        hidden = weights[0].shape[1]
        rows = 2 * self.local
        shape = (self.local, self.model)
        scratch = [pltpu.VMEM((hidden, self.model), bf16)]
        results = [(shape, f32), (shape, bf16)] + [((rows, hidden), bf16)] * 3
        return [
            self.call(mlp_kernel, results, [*pair, *weights], scratch, 6)
            for pair in (m[:2], m[2:])
        ]

    def mlp_back(self, y, saved, weights):
        hidden = weights[0].shape[1]
        rows = 2 * self.local
        shape = (self.local, self.model)
        scratch = [pltpu.VMEM((hidden, self.model), bf16)]
        results = [(shape, f32), (shape, bf16)] + [((rows, hidden), bf16)] * 2
        return [
            self.call(mlp_back_kernel, results, [*pair, *kept, *weights], scratch, 6)
            for pair, kept in ((y[:2], saved[0]), (y[2:], saved[1]))
        ]

    def gate_grads(self, m, near, far):
        hidden = near.shape[-1]
        blocks = self.blocks if self.block % 128 == 0 else 1
        shape = ((blocks, hidden, self.model // 2 // blocks), bf16)
        keep, send = self.call(
            gate_grad_kernel,
            [shape] * 2,
            [*m, near, far],
        )
        if blocks != self.blocks:
            keep, send = [
                rows.reshape(hidden, self.blocks, self.block).transpose(1, 0, 2)
                for rows in (keep, send)
            ]
        return (keep, send)

    def mlp_layout(self, rows):
        if self.block % 128 == 0:
            return rows
        hidden = rows.shape[1]
        cut = rows.reshape(self.blocks, hidden, 2, self.block).transpose(1, 2, 0, 3)
        return cut.reshape(1, hidden, self.model)

    def rows_grads(self, near, far, y):
        size = near.shape[-1]
        return self.call(
            rows_grad_kernel,
            [((size // 2, self.model), bf16)] * 2,
            [near, far, *y],
            [pltpu.VMEM((size, self.model), f32)],
        )

    def qkv_grads(self, a, joined):
        shape = ((self.blocks, self.block, 3 * self.width), bf16)
        return self.call(qkv_grad_kernel, [shape] * 2, [*a, joined], micros=4)


def routes(seq_size, group_size, slots_here):
    slots = slots_here * group_size
    parts = seq_size // slots
    result = []
    for r in range(slots_here):
        pairs = []
        for s in range(seq_size):
            for f in range(group_size):
                slot = slots_here * f + (s + r) % slots_here
                t = slot * parts + s // slots
                k = s % slots // slots_here
                pairs.append((s * group_size + f, t * group_size + k))
        result.append(pairs)
    return result


def shards(tokens, doc_bounds, w_qkv, w_out, w_gate, w_up, w_down, norm_attn, norm_mlp, out_grad):
    slots_here, block, model = tokens.shape
    seq_size = lax.axis_size(("sz", "sy"))
    group_size = lax.axis_size(("fx", "fc"))
    sz_size = seq_size // 2
    seq_at = lax.axis_index(("sz", "sy"))
    me = lax.axis_index(("fx", "fc"))
    parts = seq_size // (slots_here * group_size)
    local = slots_here * block
    width = model // group_size
    in_rows = w_qkv.shape[1]
    group_rows = in_rows * group_size
    hidden_rows = w_down.shape[1]
    hidden_here = hidden_rows * seq_size
    paths = routes(seq_size, group_size, slots_here)
    backs = [[(target, source) for source, target in pairs] for pairs in paths]

    def to_group(array):
        got = [
            lax.ppermute(pick(array, (seq_at + r) % 2), ALL, paths[r]) for r in range(slots_here)
        ]
        return in_order(seq_at // parts % 2, got[0], got[1], 0).reshape(local, model)

    def from_group(rows):
        rows = rows.astype(bf16).reshape(slots_here, block, model)
        at = seq_at // parts % 2
        got = [lax.ppermute(pick(rows, (at + r) % 2), ALL, backs[r]) for r in range(slots_here)]
        return in_order(seq_at % 2, got[0], got[1], 0).astype(f32)

    def gathered(own):
        return lax.all_gather(own, "sz", axis=0, tiled=False)

    def qkv_pieces(layer):
        pieces = w_qkv[layer].reshape(in_rows, 3, group_size, width).transpose(2, 0, 1, 3)
        return pieces.reshape(group_size, in_rows, 3 * width)

    def attention_weights(layer, mine):
        outs = w_out[layer].reshape(in_rows, group_size, width).transpose(1, 0, 2)
        own = gathered(jnp.concatenate([mine, outs.reshape(group_rows, width)], axis=1))
        other = swap_y(own[:, :, : 3 * width])
        outs = own[:, :, 3 * width :].reshape(group_size, -1, group_size, in_rows, width)
        outs = exchange(outs.transpose(0, 1, 3, 2, 4).reshape(group_size, -1, in_rows, model))
        outs = outs.transpose(1, 0, 2, 3)
        outs = in_order(group.me_y, outs, swap_y(outs), 1).reshape(width, model)
        return ([own], [other], outs)

    def mlp_weights(layer):
        def cut(weight):
            weight = weight[layer].reshape(in_rows, sz_size, 2, group_size, hidden_rows)
            return weight.transpose(3, 0, 2, 1, 4).reshape(group_size, in_rows, hidden_here)

        mine = exchange(group.hold(jnp.stack([cut(w_gate), cut(w_up)], axis=1)))
        mine = mine.transpose(1, 0, 2, 3).reshape(2 * group_rows, hidden_here).T
        if layer > 0:
            group.need(mine)
        own = gathered(mine)
        return (group.mlp_layout(own), group.mlp_layout(swap_y(own)))

    bounds = lax.ppermute(pick(doc_bounds, seq_at % 2), ALL, paths[0])
    group = Group(local, model, width, parts, bounds)
    gains = jnp.stack([norm_attn[0], norm_mlp[0], norm_attn[1], norm_mlp[1]])
    sums = (to_group(tokens),)
    first_qkv = exchange(qkv_pieces(0)).reshape(group_rows, 3 * width)
    gains = jnp.stack(by_distance(jnp.stack(gather_near(gains.astype(f32)))))
    gains = gains.transpose(1, 0, 2).reshape(4, sz_size, 1, 1, in_rows)
    gains = in_order(lax.axis_index("fx"), gains, swap_x(gains), 2)[:, :, :, 0]
    gains = in_order(lax.axis_index("fc"), gains, swap_core(gains), 3)
    gains = gains.reshape(4, sz_size * group_rows)
    gains = jnp.concatenate([gains, swap_y(gains)], axis=1)
    gains = [gains[i : i + 1] for i in range(4)]

    attention = [attention_weights(0, first_qkv)]
    mlps, downs = [], None
    upstream = to_group(out_grad)

    saved = []
    first = None
    for layer in range(LAYERS):
        entry, a = group.norm(sums, gains[2 * layer])
        if layer == 0:
            gates = [mlp_weights(0)]
            downs = gathered(jnp.concatenate([w_down[0], w_down[1]]))
            cut = slice(0, hidden_rows), slice(hidden_rows, 2 * hidden_rows)
            downs = [downs[:, at].reshape(-1, model) for at in cut]
            downs = [(own, swap_y(own)) for own in downs]
            next_qkv = exchange(group.hold(qkv_pieces(1))).reshape(group_rows, 3 * width)
        else:
            group.need(gates[1][0], downs[1][1])
        a = spread(a)
        partial, kept, out, first = group.attend(a, attention[layer], first)
        if layer == 0:
            group.need(next_qkv)
            attention.append(attention_weights(1, next_qkv))
        else:
            group.need(gates[1][1])
        middle, m = group.norm((entry, *group.reduce_pieces(partial)), gains[2 * layer + 1])
        m = spread(m)
        if layer == 0:
            gates.append(mlp_weights(1))
        mlps.append(gates[layer] + downs[layer])
        near, far = group.mlp(m, mlps[layer])
        if layer == 0:
            group.need(attention[1][1][0], attention[1][2])
        sums = (middle, *group.reduce_pieces((*near[:2], *far[:2])))
        saved.append((entry, a, kept, out, middle, m, near[2:], far[2:]))
    valid = group.valid()
    hidden_out = from_group(group.plain_sum(sums) * valid)

    upstream = upstream.astype(f32) * valid
    low = upstream.astype(bf16)
    carry = None
    grads = [None] * LAYERS
    gain_grads = [None] * (2 * LAYERS)

    def out_rows(outs):
        if parts == 1:
            rows = group.add(outs[0], outs[1])
        else:
            rows = group.add(*outs)
        rows = rows.reshape(-1, group_size, in_rows, model)
        return exchange(rows.transpose(1, 0, 2, 3)).reshape(sz_size, in_rows, model)

    def swap_outs(keep, send):
        if parts == 1:
            return (keep, swap_y(send))
        both = in_order(group.me_y, keep, send, 0).reshape(-1, 2, group_rows, model)
        return (pick(both, group.me_y, 1), swap_y(pick(both, 1 - group.me_y, 1)))

    def hand_out(layer, pair, down, qkv, rows):
        pair = pair.T.reshape(2, group_size, in_rows, hidden_here).transpose(1, 0, 2, 3)
        pair = exchange(pair)
        pair = pair.reshape(group_size, 2, in_rows, 2, sz_size, hidden_rows)
        pair = pair.transpose(1, 2, 4, 3, 0, 5).reshape(2, in_rows, -1)
        qkv = exchange(qkv.reshape(group_size, in_rows, 3 * width))
        qkv = qkv.reshape(group_size, in_rows, 3, width)
        qkv = qkv.transpose(1, 2, 0, 3).reshape(in_rows, 3 * model)
        grads[layer] = (qkv, rows, pair[0], pair[1], down)

    half = 2 * local
    waiting = None
    for layer in reversed(range(LAYERS)):
        last = layer == 0
        entry, a, kept, out, middle, m, near, far = saved[layer]
        y = spread(low)
        if waiting is not None:
            pair, qkv, down, outs = waiting
            qkv = scattered(group.add(*qkv))
        near_back, far_back = group.mlp_back(y, (near[:2], far[:2]), mlps[layer])
        partial = group.reduce_pieces((*near_back[:2], *far_back[:2]))
        keep, send = group.gate_grads(m, near_back[2], far_back[2])
        gate = (keep, swap_y(send))
        if waiting is not None:
            down = group.add(*down).reshape(sz_size, hidden_rows, model)
            rows = scattered(jnp.concatenate([down, out_rows(outs)], axis=1))
        down_keep, down_send = group.rows_grads(near[2], far[2], y)
        upstream, low, gain_grads[2 * layer + 1] = group.norm_back(
            upstream, partial, middle, gains[2 * layer + 1]
        )
        y2 = spread(low)
        keep, send = group.gate_grads(m, near_back[3], far_back[3])
        up = (keep, swap_y(send))
        group.need(gate[1])
        partial, joined, value_grad = group.attend_back(y2, attention[layer], kept, carry, last)
        if not last:
            carry = value_grad if carry is None else carry + value_grad
        partial = group.reduce_pieces(partial)
        keep, send = group.qkv_grads(a, joined)
        qkv_sums = (keep, swap_y(send))
        down_sums = (down_keep, swap_y(down_send))
        if waiting is not None:
            done = [pair, qkv, rows]
        pair = scattered(group.add_pair(gate, up))
        outs = swap_outs(*group.rows_grads(out[:half], out[half:], y2))
        upstream, low, gain_grads[2 * layer] = group.norm_back(
            upstream, partial, entry, gains[2 * layer]
        )
        waiting = (pair, qkv_sums, down_sums, outs)
    pair, qkv, down, outs = waiting
    qkv = scatter_near(by_distance(group.add(*qkv))).astype(bf16)
    down = group.add(*down).reshape(sz_size, hidden_rows, model)
    rows = out_rows(outs)
    extra = sum_near(jnp.concatenate(gain_grads)).reshape(2 * LAYERS, sz_size, group_rows)
    extra = extra.astype(bf16).transpose(1, 0, 2)
    extra = jnp.pad(extra, ((0, 0), (0, 8 - 2 * LAYERS), (0, model - group_rows)))
    rows = scattered(jnp.concatenate([down, rows, extra], axis=1))
    down, rows = rows[:hidden_rows], rows[hidden_rows:]
    gain_sums = rows[in_rows : in_rows + 2 * LAYERS].astype(f32)
    gain_sums = lax.dynamic_slice(gain_sums, (0, me * in_rows), (2 * LAYERS, in_rows))
    pair_1, qkv_1, rows_1 = [group.hold(one) for one in done]
    value_grad = group.hold(value_grad)
    hand_out(1, pair_1, rows_1[:hidden_rows], qkv_1, rows_1[hidden_rows:])
    hand_out(0, pair, down, qkv, rows[:in_rows])
    pieces = value_grad.astype(bf16).reshape(group_size, local, width)
    if parts != 1:
        order = me ^ jnp.arange(group_size, dtype=jnp.int32)
        pieces = jnp.take(pieces, order, axis=0)
    first_grad = exchange(pieces).transpose(1, 0, 2).reshape(local, model)
    stacked = [
        jnp.stack([grads[layer][member].astype(f32) for layer in range(LAYERS)])
        for member in range(5)
    ]
    return (
        hidden_out,
        from_group(upstream),
        *stacked,
        gain_sums[0::2],
        gain_sums[1::2],
        from_group(first_grad),
    )


def solution(mesh):
    seq, fsdp = mesh.shape["seq"], mesh.shape["fsdp"]
    inner = Mesh(mesh.devices.reshape(seq // 2, 2, fsdp // 2, 2), ALL)
    rows = P(("fx", "fc"), ("sz", "sy"), None)
    weight, gain = P(None, ALL, None), P(None, ALL)
    in_specs = (rows, P(("fx", "fc"), None)) + (weight,) * 5 + (gain,) * 2 + (rows,)
    out_specs = (rows, rows) + (weight,) * 5 + (gain,) * 2 + (rows,)
    return jax.shard_map(
        shards, mesh=inner, in_specs=in_specs, out_specs=out_specs, check_vma=False
    )
```

```python
import functools

import jax
import jax.numpy as jnp
from jax import lax
from jax.experimental import pallas as pl
from jax.experimental.pallas import tpu as pltpu
from jax.sharding import Mesh, PartitionSpec as P

HD = 64
LAYERS = 2
epsilon = 1e-05
masked_score = -1e30
SCALE = 0.125 * 1.4426950408889634
bf16 = jnp.bfloat16
f32 = jnp.float32

ALL = ("sz", "sy", "fx", "fc")
SWAP = ((0, 1), (1, 0))
VMEM_LIMIT = 24 * 1024 * 1024


def dot(left, right):
    return jnp.dot(left, right, preferred_element_type=f32)


def dot_rows(left, right):
    return lax.dot_general(left, right, (((0,), (0,)), ((), ())), preferred_element_type=f32)


def dot_cols(left, right):
    return lax.dot_general(left, right, (((1,), (1,)), ((), ())), preferred_element_type=f32)


def swap_core(value):
    return lax.ppermute(value, "fc", SWAP)


def swap_x(value):
    return lax.ppermute(value, "fx", SWAP)


def swap_y(value):
    return lax.ppermute(value, "sy", SWAP)


def pick(array, index, axis=0):
    return lax.dynamic_index_in_dim(array, index, axis, keepdims=False)


def in_order(flag, first, second, axis):
    return jnp.where(
        flag == 0, jnp.stack([first, second], axis), jnp.stack([second, first], axis)
    )


def exchange(pieces):
    fx, fc = lax.axis_index("fx"), lax.axis_index("fc")
    pieces = pieces.reshape((2, 2) + pieces.shape[1:])
    got = swap_x(pick(pieces, 1 - fx))
    both = in_order(fx, pick(pieces, fx), got, 0)
    got = swap_core(pick(both, 1 - fc, 1))
    both = in_order(fc, pick(both, fc, 1), got, 1)
    return both.reshape((4,) + both.shape[2:])


def sum_near(value):
    value = value + swap_x(value)
    value = value + swap_core(value)
    half = value.shape[1] // 2
    got = swap_y(value)
    return value[:, :half] + got[:, half:]


def steps_z():
    size = lax.axis_size("sz")
    return [(d, [(i, i ^ d) for i in range(size)]) for d in range(1, size)]


def gather_near(block):
    return [block] + [lax.ppermute(block, "sz", pairs) for _, pairs in steps_z()]


def scatter_near(blocks):
    total = blocks[0].astype(f32)
    for d, pairs in steps_z():
        total = total + lax.ppermute(blocks[d], "sz", pairs).astype(f32)
    return total


def by_distance(rows):
    at = lax.axis_index("sz")
    return [pick(rows, at ^ d) for d in range(rows.shape[0])]


def scattered(total):
    return lax.psum_scatter(total, "sz", scatter_dimension=0, tiled=False)


def spread(value):
    over = swap_x(value)
    return (value, swap_core(value), over, swap_core(over))


def kernel_call(body, results, scalars, operands, scratch, after, flops):
    count, extra = len(operands), len(after)

    def whole(scalars_ref, *refs):
        body(scalars_ref, *refs[:count], *refs[count + extra :])

    vmem = pl.BlockSpec(memory_space=pltpu.VMEM)
    return pl.pallas_call(
        whole,
        out_shape=[shape_of(*one) for one in results],
        in_specs=[pl.BlockSpec(memory_space=pltpu.SMEM)]
        + [vmem] * count
        + [pl.BlockSpec(memory_space=pl.ANY)] * extra,
        out_specs=[vmem] * len(results),
        scratch_shapes=list(scratch),
        compiler_params=pltpu.CompilerParams(vmem_limit_bytes=VMEM_LIMIT),
        cost_estimate=pl.CostEstimate(
            flops=1, bytes_accessed=1, transcendentals=0
        ),
    )(scalars, *operands, *after)


def shape_of(shape, dtype):
    return jax.ShapeDtypeStruct(shape, dtype)


def block_pairs(scalars, width):
    half, me_y = width // 256, scalars[3]
    for i in range(half):
        yield (i * 128, pl.multiple_of((2 * i + me_y) * 128, 128))
        yield ((half + i) * 128, pl.multiple_of((2 * i + 1 - me_y) * 128, 128))


def norm_kernel(added, scalars, *refs):
    inputs, (gain_ref, sum_ref, out_ref) = refs[:added], refs[added:]
    total = inputs[0][...].astype(f32)
    for ref in inputs[1:]:
        total += (ref[...] if len(ref.shape) == 2 else ref[0]).astype(f32)
    sum_ref[...] = total
    inverse = lax.rsqrt(jnp.mean(total * total, axis=-1, keepdims=True) + epsilon)
    for local, natural in block_pairs(scalars, sum_ref.shape[1]):
        normed = sum_ref[:, pl.ds(natural, 128)] * inverse
        out_ref[:, local : local + 128] = (normed * gain_ref[:, local : local + 128]).astype(bf16)


def norm_back_kernel(scalars, up_ref, d0, d1, d2, z_ref, gain_ref, up_out, low_out, gain_out, work):
    z = z_ref[...]
    inverse = lax.rsqrt(jnp.mean(z * z, axis=-1, keepdims=True) + epsilon)
    for local, natural in block_pairs(scalars, z.shape[1]):
        here = slice(local, local + 128)
        core = d1[:, here] if len(d1.shape) == 2 else d1[0, :, here]
        dy = d0[:, here] + core.astype(f32) + d2[:, here].astype(f32)
        normed = z_ref[:, pl.ds(natural, 128)] * inverse
        gain_out[:, here] = jnp.sum(dy * normed, axis=0, keepdims=True)
        work[:, pl.ds(natural, 128)] = dy * gain_ref[:, here]
    scaled = work[...]
    normed = z * inverse
    mean = jnp.mean(scaled * normed, axis=-1, keepdims=True)
    up = up_ref[...] + inverse * (scaled - normed * mean)
    up_out[...] = up
    low_out[...] = up.astype(bf16)


def add_kernel(scalars, left, right, out_ref):
    out_ref[...] = (left[...].astype(f32) + right[...].astype(f32)).astype(out_ref.dtype)


def add_second_kernel(scalars, left, right, out_ref):
    out_ref[...] = (left[...] + right[1].astype(f32)).astype(out_ref.dtype)


def add_pair_kernel(scalars, left, right, second_left, second_right, out_ref):
    size = left.shape[2]
    out_ref[:, :, :size] = (left[...].astype(f32) + right[...].astype(f32)).astype(bf16)
    out_ref[:, :, size:] = (second_left[...].astype(f32) + second_right[...].astype(f32)).astype(bf16)


def hold_kernel(scalars, value, out_ref):
    out_ref[...] = value[...]


def partner(rows):
    lane = lax.broadcasted_iota(jnp.int32, rows.shape, 1)
    return jnp.where(lane % 64 < 32, pltpu.roll(rows, 96, 1), pltpu.roll(rows, 32, 1))


def block_mask(block, rows, start, end):
    shape = (rows, (block + 1) * rows)
    query = block * rows + lax.broadcasted_iota(jnp.int32, (rows, 1), 0)
    lowest = jnp.where(query < start, 0, jnp.where(query < end, start, end))
    key = lax.broadcasted_iota(jnp.int32, shape, 1)
    return (key <= query) & (key >= lowest)


def weigh_rows(scores, allowed):
    scores = jnp.where(allowed, scores * SCALE, masked_score)
    weights = jnp.exp2(scores - jnp.max(scores, axis=-1, keepdims=True))
    return (weights, 1.0 / jnp.sum(weights, axis=-1, keepdims=True))


def softmax_rows(scores, allowed):
    scores = jnp.where(allowed, scores * 0.125, masked_score)
    weights = jnp.exp(scores - jnp.max(scores, axis=-1, keepdims=True))
    return weights * (1.0 / jnp.sum(weights, axis=-1, keepdims=True))


def flat(ref, first, last):
    value = ref[:, first:last, :]
    return value.reshape(-1, value.shape[-1])


def rows_of(refs, columns):
    values = []
    for ref in refs:
        if len(ref.shape) == 3:
            values.append(ref[:, :, :columns].reshape(-1, columns))
        else:
            values.append(ref[:, :columns])
    return values[0] if len(values) == 1 else jnp.concatenate(values, axis=0)


def place(ref, me_y, own, other):
    half = own.shape[0]
    ref[pl.ds(pl.multiple_of(me_y * half, half), half), :] = own
    ref[pl.ds(pl.multiple_of((1 - me_y) * half, half), half), :] = other


def attention_kernel(blend, count, scalars, a0, a1, a2, a3, *refs):
    own, other, refs = refs[:count], refs[count : 2 * count], refs[2 * count :]
    cos_ref, sin_ref, refs = refs[0], refs[1], refs[2:]
    if blend:
        first_ref, q_ref, k_ref, v_ref, o_ref = refs
    else:
        q_ref, k_ref, v_ref, o_ref, first_ref = refs
    me, start, end = scalars[0], scalars[1], scalars[2]
    total, width = q_ref.shape
    rows = total // 4
    here_w, there_w = rows_of(own, 3 * width), rows_of(other, 3 * width)
    half = here_w.shape[0]
    for i, a_ref in enumerate((a0, a1, a2, a3)):
        part = dot(a_ref[:, :half], here_w) + dot(a_ref[:, half:], there_w)
        here = slice(i * rows, (i + 1) * rows)
        there = pl.ds(pl.multiple_of((me ^ i) * rows, rows), rows)
        cosine, sine = cos_ref[here, :], sin_ref[here, :]
        for j in range(width // 128):
            for into, at in ((q_ref, 0), (k_ref, width)):
                piece = part[:, at + j * 128 : at + (j + 1) * 128]
                turned = piece * cosine + partner(piece) * sine
                into[there, j * 128 : (j + 1) * 128] = turned.astype(bf16)
        value = part[:, 2 * width :]
        if blend:
            value = 0.5 * value + 0.5 * first_ref[there, :]
        else:
            first_ref[there, :] = value
        v_ref[there, :] = value.astype(bf16)
    lane = lax.broadcasted_iota(jnp.int32, (rows, 128), 1)
    for b in range(4):
        allowed = block_mask(b, rows, start, end)
        there = pl.ds(pl.multiple_of((me ^ b) * rows, rows), rows)
        for j in range(width // 128):
            columns = slice(j * 128, (j + 1) * 128)
            query = q_ref[b * rows : (b + 1) * rows, columns]
            keys = k_ref[: (b + 1) * rows, columns]
            values = v_ref[: (b + 1) * rows, columns]
            outs = []
            for h in range(2):
                one = jnp.where(lane // 64 == h, query, jnp.zeros_like(query))
                weights, share = weigh_rows(dot_cols(one, keys), allowed)
                outs.append(dot(weights.astype(bf16), values) * share)
            o_ref[there, columns] = jnp.where(lane < 64, outs[0], outs[1]).astype(bf16)


def out_kernel(scalars, o_ref, out_w, near, far, cores):
    rows = near.shape[0]
    cores[1] = dot(o_ref[3 * rows :, :], out_w[...]).astype(bf16)
    cores[0] = dot(o_ref[rows : 2 * rows, :], out_w[...]).astype(bf16)
    far[...] = dot(o_ref[2 * rows : 3 * rows, :], out_w[...])
    near[...] = dot(o_ref[:rows, :], out_w[...])


def attention_back_kernel(last, count, scalars, y0, y1, y2, y3, *refs):
    own, other, refs = refs[:count], refs[count : 2 * count], refs[2 * count :]
    out_w, cos_ref, sin_ref, q_ref, k_ref, v_ref = refs[:6]
    refs = refs[6:]
    if last:
        carry_ref, near, far, cores, d_ref, dv_ref, dk_sum, dv_sum, up_ref = refs
    else:
        near, far, cores, d_ref, dv_ref, dk_sum, dv_sum, up_ref = refs
    me, start, end = scalars[0], scalars[1], scalars[2]
    total, width = q_ref.shape
    rows = total // 4
    for i, y_ref in enumerate((y0, y1, y2, y3)):
        there = pl.ds(pl.multiple_of((me ^ i) * rows, rows), rows)
        up_ref[there, :] = dot_cols(y_ref[...], out_w[...]).astype(bf16)
    lane = lax.broadcasted_iota(jnp.int32, (rows, 128), 1)
    dk_sum[...] = jnp.zeros_like(dk_sum)
    dv_sum[...] = jnp.zeros_like(dv_sum)
    for b in range(4):
        allowed = block_mask(b, rows, start, end)
        there = pl.ds(pl.multiple_of((me ^ b) * rows, rows), rows)
        upto = slice(0, (b + 1) * rows)
        cosine, sine = cos_ref[there, :], sin_ref[there, :]
        for j in range(width // 128):
            columns = slice(j * 128, (j + 1) * 128)
            query = q_ref[b * rows : (b + 1) * rows, columns]
            keys, values = k_ref[upto, columns], v_ref[upto, columns]
            up = up_ref[b * rows : (b + 1) * rows, columns]
            dq, dk, dv = [], [], []
            for h in range(2):
                mine = lane // 64 == h
                one = jnp.where(mine, query, jnp.zeros_like(query))
                one_up = jnp.where(mine, up, jnp.zeros_like(up))
                weights, share = weigh_rows(dot_cols(one, keys), allowed)
                chance = weights * share
                back = dot_cols(one_up, values)
                delta = jnp.sum(chance * back, axis=-1, keepdims=True)
                score = (chance * (back - delta)).astype(bf16)
                dq.append(dot(score, keys))
                dk.append(dot_rows(score, one * 0.125))
                dv.append(dot_rows(chance.astype(bf16), one_up))
            dk_sum[upto, columns] += dk[0] + dk[1]
            dv_sum[upto, columns] += dv[0] + dv[1]
            dq = jnp.where(lane < 64, dq[0], dq[1]) * 0.125
            d_ref[there, columns] = (dq * cosine - partner(dq) * sine).astype(bf16)
    for b in range(4):
        there = pl.ds(pl.multiple_of((me ^ b) * rows, rows), rows)
        here = slice(b * rows, (b + 1) * rows)
        cosine, sine = cos_ref[there, :], sin_ref[there, :]
        for j in range(width // 128):
            dk = dk_sum[here, j * 128 : (j + 1) * 128]
            dk = dk * cosine - partner(dk) * sine
            d_ref[there, width + j * 128 : width + (j + 1) * 128] = dk.astype(bf16)
        dv = dv_sum[here, :]
        dv = dv + carry_ref[here, :] if last else 0.5 * dv
        dv_ref[here, :] = dv
        d_ref[there, 2 * width : 3 * width] = dv.astype(bf16)
    here_w, there_w = rows_of(own, 3 * width), rows_of(other, 3 * width)
    half = here_w.shape[0]
    for at, weight in ((slice(0, half), here_w), (slice(half, 2 * half), there_w)):
        for i in range(4):
            total_d = dot_cols(d_ref[i * rows : (i + 1) * rows, :], weight)
            if i % 2:
                cores[i // 2, :, at] = total_d.astype(bf16)
            else:
                (far if i else near)[:, at] = total_d


def mlp_halves(ref):
    size = ref.shape[2] // 2
    blocks = range(ref.shape[0])
    return [
        jnp.concatenate([ref[z, :, at : at + size] for z in blocks], axis=1) for at in (0, size)
    ]


def mlp_kernel(scalars, m0, m1, own, other, down_own, down_other, p0, p1, g_ref, u_ref, z_ref, down):
    rows = m0.shape[0]
    place(down, scalars[3], down_own[...], down_other[...])
    gate_own, up_own = mlp_halves(own)
    gate_other, up_other = mlp_halves(other)
    half = gate_own.shape[1]
    for i, (m_ref, p_ref) in enumerate(((m0, p0), (m1, p1))):
        here = slice(i * rows, (i + 1) * rows)
        left, right = m_ref[:, :half], m_ref[:, half:]
        gate = dot_cols(left, gate_own) + dot_cols(right, gate_other)
        up = dot_cols(left, up_own) + dot_cols(right, up_other)
        active = (jax.nn.silu(gate) * up).astype(bf16)
        g_ref[here, :] = gate.astype(bf16)
        u_ref[here, :] = up.astype(bf16)
        z_ref[here, :] = active
        p_ref[...] = dot(active, down[...]).astype(p_ref.dtype)


def mlp_back_kernel(scalars, y0, y1, g_ref, u_ref, own, other, down_own, down_other, p0, p1, dg_ref, du_ref, down):
    rows = y0.shape[0]
    place(down, scalars[3], down_own[...], down_other[...])
    gate_own, up_own = mlp_halves(own)
    gate_other, up_other = mlp_halves(other)
    half = gate_own.shape[1]
    for i, (y_ref, p_ref) in enumerate(((y0, p0), (y1, p1))):
        here = slice(i * rows, (i + 1) * rows)
        back = dot_cols(y_ref[...], down[...])
        gate, up = g_ref[here, :].astype(f32), u_ref[here, :].astype(f32)
        sigmoid = jax.nn.sigmoid(gate)
        dg = (back * up * sigmoid * (1.0 + gate * (1.0 - sigmoid))).astype(bf16)
        du = (back * (gate * sigmoid)).astype(bf16)
        dg_ref[here, :] = dg
        du_ref[here, :] = du
        p_ref[:, :half] = (dot(dg, gate_own) + dot(du, up_own)).astype(p_ref.dtype)
        p_ref[:, half:] = (dot(dg, gate_other) + dot(du, up_other)).astype(p_ref.dtype)


def gate_grad_kernel(scalars, m0, m1, m2, m3, near, far, keep, send):
    rows = m0.shape[0]
    blocks, size = keep.shape[0], keep.shape[2]
    half = blocks * size
    for into, columns in ((send, slice(half, 2 * half)), (keep, slice(0, half))):
        total = dot_rows(near[:rows, :], m0[:, columns])
        total += dot_rows(near[rows:, :], m1[:, columns])
        total += dot_rows(far[:rows, :], m2[:, columns])
        total += dot_rows(far[rows:, :], m3[:, columns])
        for z in range(blocks):
            into[z] = total[:, z * size : (z + 1) * size].astype(bf16)


def rows_grad_kernel(scalars, left_near, left_far, y0, y1, y2, y3, keep, send, work):
    rows = y0.shape[0]
    half = keep.shape[0]
    work[...] = dot_rows(left_near[:rows, :], y0[...]) + dot_rows(left_near[rows:, :], y1[...])
    work[...] += dot_rows(left_far[:rows, :], y2[...]) + dot_rows(left_far[rows:, :], y3[...])
    me_y = scalars[3]
    keep[...] = work[pl.ds(pl.multiple_of(me_y * half, half), half), :].astype(bf16)
    send[...] = work[pl.ds(pl.multiple_of((1 - me_y) * half, half), half), :].astype(bf16)


def qkv_grad_kernel(scalars, a0, a1, a2, a3, d_ref, keep, send):
    rows = a0.shape[0]
    blocks, size = keep.shape[0], keep.shape[1]
    half = blocks * size
    for into, columns in ((send, slice(half, 2 * half)), (keep, slice(0, half))):
        total = dot_rows(a0[:, columns], d_ref[:rows, :])
        for i, a_ref in ((1, a1), (2, a2), (3, a3)):
            total += dot_rows(a_ref[:, columns], d_ref[i * rows : (i + 1) * rows, :])
        into[...] = total.astype(bf16).reshape(blocks, size, -1)


def turn(rows, cosine, sine):
    total, width = rows.shape
    halves = rows.reshape(total, width // HD, 2, HD // 2)
    cosine = cosine[:, :HD].reshape(total, 1, 2, HD // 2)
    sine = sine[:, :HD].reshape(total, 1, 2, HD // 2)
    return (halves * cosine + halves[:, :, ::-1] * sine).reshape(total, width)


class Group:
    def __init__(self, local, model, width, parts, bounds):
        self.local, self.model, self.width, self.parts = local, model, width, parts
        self.total = total = 4 * local
        self.me_y = lax.axis_index("sy")
        self.blocks = lax.axis_size("sz")
        me = lax.axis_index(("fx", "fc"))
        self.part = lax.axis_index(("sz", "sy")) % parts
        order = (me ^ jnp.arange(4, dtype=jnp.int32)) * local
        self.inner = (order[:, None] + jnp.arange(local, dtype=jnp.int32)[None, :]).reshape(total)
        self.start, self.end = bounds[0], bounds[1]
        self.index = index = self.part * total + self.inner
        self.me_z = lax.axis_index("sz")
        self.scalars = jnp.stack([me, self.start, self.end, self.me_y, self.me_z]).astype(jnp.int32)
        base = jnp.where(index < self.start, 0, jnp.where(index < self.end, self.start, self.end))
        frequency = 10000.0 ** (-jnp.arange(HD // 2, dtype=f32) * 2.0 / HD)
        angles = (index - base).astype(f32)[:, None] * frequency[None, :]
        cosine, sine = jnp.cos(angles), jnp.sin(angles)
        self.cosine = jnp.concatenate([cosine] * 4, axis=1)
        self.sine = jnp.concatenate([-sine, sine] * 2, axis=1)
        self.block = model // (2 * self.blocks)
        self.latest, self.needed = None, []

    def call(self, body, shapes, operands, scratch=(), micros=1):
        after = self.needed + ([] if self.latest is None else [self.latest])
        self.needed = []
        flops = int(micros * 1e9)
        got = kernel_call(body, shapes, self.scalars, operands, scratch, after, flops)
        self.latest = got[-1]
        return got

    def add(self, left, right):
        return self.call(add_kernel, [(left.shape, bf16)], [left, right])[0]

    def need(self, *values):
        self.needed += values

    def add_pair(self, first, second):
        shape = (*first[0].shape[:2], 2 * first[0].shape[2])
        if self.block % 128:
            sums = [self.add(*one) for one in (first, second)]
            return jnp.concatenate(sums, axis=2)
        return self.call(add_pair_kernel, [(shape, bf16)], [*first, *second])[0]

    def hold(self, value):
        return self.call(hold_kernel, [(value.shape, value.dtype)], [value])[0]

    def reduce_pieces(self, pieces):
        if len(pieces) == 3:
            got = swap_core(pieces[2])
            out = self.call(
                add_second_kernel,
                [(pieces[1].shape, bf16)],
                [pieces[1], got],
            )[0]
            return (pieces[0], got, swap_x(out))
        got = swap_core(pieces[3])
        out = self.call(
            add_kernel, [(got.shape, bf16)], [pieces[2], got]
        )[0]
        return (pieces[0], swap_core(pieces[1]), swap_x(out))

    def sum_y(self, keep, send):
        return self.add(keep, send)

    def valid(self):
        return (self.index[: self.local] < self.end).astype(f32)[:, None]

    def to_local(self, rows):
        cut = rows.reshape(rows.shape[0], self.blocks, 2, self.block)
        pair = in_order(self.me_y, cut[:, :, 0], cut[:, :, 1], 1)
        return pair.reshape(rows.shape[0], self.model)

    def to_natural(self, rows):
        cut = rows.reshape(rows.shape[0], 2, self.blocks, self.block)
        cut = in_order(self.me_y, cut[:, 0], cut[:, 1], 2)
        return cut.reshape(rows.shape[0], self.model)

    def plain_sum(self, pieces):
        return sum((one if one.ndim == 2 else one[0]).astype(f32) for one in pieces)

    def norm(self, pieces, gain):
        if self.block % 128 == 0:
            shape = (self.local, self.model)
            return self.call(
                functools.partial(norm_kernel, len(pieces)),
                [(shape, f32), (shape, bf16)],
                [*pieces, gain],
            )
        total = self.plain_sum(pieces)
        inverse = lax.rsqrt(jnp.mean(total * total, axis=-1, keepdims=True) + epsilon)
        return (total, (self.to_local(total * inverse) * gain).astype(bf16))

    def norm_back(self, up, pieces, z, gain):
        if self.block % 128 == 0:
            shape = (self.local, self.model)
            return self.call(
                norm_back_kernel,
                [(shape, f32), (shape, bf16), ((1, self.model), f32)],
                [up, *pieces, z, gain],
                [pltpu.VMEM(shape, f32)],
            )
        dy = self.plain_sum(pieces)
        inverse = lax.rsqrt(jnp.mean(z * z, axis=-1, keepdims=True) + epsilon)
        normed = z * inverse
        gain_grad = jnp.sum(dy * self.to_local(normed), axis=0, keepdims=True)
        scaled = self.to_natural(dy * gain)
        mean = jnp.mean(scaled * normed, axis=-1, keepdims=True)
        up = up + inverse * (scaled - normed * mean)
        return (up, up.astype(bf16), gain_grad)

    def pieces(self):
        shape = (self.local, self.model)
        return [(shape, f32), (shape, f32), ((2, *shape), bf16)]

    def cut(self, rows):
        cut = rows.reshape(4, self.local, -1)
        return (cut[0], cut[2], cut[1::2].astype(bf16))

    def attend(self, a, weights, first):
        total, width = self.total, self.width
        tables = [self.cosine, self.sine]
        own, other, out_w = weights
        if self.parts == 1:
            results = [((total, width), bf16)] * 4
            operands = [*a, *own, *other, *tables]
            if first is None:
                results += [((total, width), f32)]
            else:
                operands += [first]
            got = self.call(
                functools.partial(attention_kernel, first is not None, len(own)),
                results,
                operands,
                micros=12,
            )
            partial = self.call(out_kernel, self.pieces(), [got[3], out_w], micros=3)
            return (partial, got[:3], got[3], got[4] if first is None else first)
        own, other = self.plain(own), self.plain(other)
        rows = jnp.concatenate(a)
        part = dot(rows[:, : own.shape[0]], own) + dot(rows[:, own.shape[0] :], other)
        query = turn(part[:, :width], *tables).astype(bf16)
        key = turn(part[:, width : 2 * width], *tables).astype(bf16)
        value = part[:, 2 * width :]
        if first is None:
            first = value
        else:
            value = 0.5 * value + 0.5 * first
        value = value.astype(bf16)

        def one(items):
            q, k, v = items
            return dot(softmax_rows(dot_cols(q, k), self.allowed()).astype(bf16), v)

        packed = (self.heads(query), self.heads(self.slot(key)), self.heads(self.slot(value)))
        out = self.rows(lax.map(one, packed)).astype(bf16)
        return (self.cut(dot(out, out_w)), (query, key, value), out, first)

    def attend_back(self, y, weights, saved, carry, last):
        total, width = self.total, self.width
        own, other, out_w = weights
        if self.parts == 1:
            operands = [*y, *own, *other, out_w, self.cosine, self.sine, *saved]
            if last:
                operands += [carry]
            got = self.call(
                functools.partial(attention_back_kernel, last, len(own)),
                self.pieces() + [((total, 3 * width), bf16), ((total, width), f32)],
                operands,
                [pltpu.VMEM((total, width), f32)] * 2 + [pltpu.VMEM((total, width), bf16)],
                micros=20,
            )
            return (got[:3], got[3], got[4])
        own, other = self.plain(own), self.plain(other)
        query, key, value = saved
        up = dot_cols(jnp.concatenate(y), out_w).astype(bf16)

        def one(items):
            q, k, v, u = items
            chance = softmax_rows(dot_cols(q, k), self.allowed())
            back = dot_cols(u, v)
            delta = jnp.sum(chance * back, axis=-1, keepdims=True)
            score = (chance * (back - delta) * 0.125).astype(bf16)
            return (dot(score, k), dot_rows(score, q), dot_rows(chance.astype(bf16), u))

        packed = (query, self.slot(key), self.slot(value), up)
        dq, dk, dv = lax.map(one, tuple(self.heads(rows) for rows in packed))
        dk, dv = self.collect(self.rows(dk)), self.collect(self.rows(dv))
        dv = dv + carry if last else 0.5 * dv
        back_turn = functools.partial(turn, cosine=self.cosine, sine=-self.sine)
        joined = jnp.concatenate([back_turn(self.rows(dq)), back_turn(dk), dv], axis=1)
        joined = joined.astype(bf16)
        sums = jnp.concatenate([dot_cols(joined, own), dot_cols(joined, other)], axis=1)
        return (self.cut(sums), joined, dv)

    def plain(self, blocks):
        wide = 3 * self.width
        return jnp.concatenate([block[..., :wide].reshape(-1, wide) for block in blocks])

    def rotate_parts(self, value, shift):
        if shift % self.parts == 0:
            return value
        pairs = []
        for t in range(lax.axis_size(("sz", "sy"))):
            head = t - t % self.parts
            pairs.append((head + (t + shift) % self.parts, t))
        return lax.ppermute(value, ("sz", "sy"), pairs)

    def slot(self, value):
        return jnp.concatenate([self.rotate_parts(value, r) for r in range(self.parts)])

    def heads(self, rows):
        return rows.reshape(rows.shape[0], -1, HD).transpose(1, 0, 2)

    def rows(self, heads):
        return heads.transpose(1, 0, 2).reshape(heads.shape[1], -1)

    def allowed(self):
        key = jnp.concatenate(
            [(self.part + r) % self.parts * self.total + self.inner for r in range(self.parts)]
        )
        query = self.index[:, None]
        lowest = jnp.where(
            query < self.start, 0, jnp.where(query < self.end, self.start, self.end)
        )
        return (key[None, :] <= query) & (key[None, :] >= lowest)

    def collect(self, slot_rows):
        pieces = slot_rows.reshape(self.parts, self.total, -1)
        result = pieces[0]
        for r in range(1, self.parts):
            result = result + self.rotate_parts(pieces[r].astype(bf16), -r).astype(f32)
        return result

    def mlp(self, m, weights):
        hidden = weights[0].shape[1]
        rows = 2 * self.local
        shape = (self.local, self.model)
        scratch = [pltpu.VMEM((hidden, self.model), bf16)]
        results = [(shape, f32), (shape, bf16)] + [((rows, hidden), bf16)] * 3
        return [
            self.call(mlp_kernel, results, [*pair, *weights], scratch, 6)
            for pair in (m[:2], m[2:])
        ]

    def mlp_back(self, y, saved, weights):
        hidden = weights[0].shape[1]
        rows = 2 * self.local
        shape = (self.local, self.model)
        scratch = [pltpu.VMEM((hidden, self.model), bf16)]
        results = [(shape, f32), (shape, bf16)] + [((rows, hidden), bf16)] * 2
        return [
            self.call(mlp_back_kernel, results, [*pair, *kept, *weights], scratch, 6)
            for pair, kept in ((y[:2], saved[0]), (y[2:], saved[1]))
        ]

    def gate_grads(self, m, near, far):
        hidden = near.shape[-1]
        blocks = self.blocks if self.block % 128 == 0 else 1
        shape = ((blocks, hidden, self.model // 2 // blocks), bf16)
        keep, send = self.call(
            gate_grad_kernel,
            [shape] * 2,
            [*m, near, far],
        )
        if blocks != self.blocks:
            keep, send = [
                rows.reshape(hidden, self.blocks, self.block).transpose(1, 0, 2)
                for rows in (keep, send)
            ]
        return (keep, send)

    def mlp_layout(self, rows):
        if self.block % 128 == 0:
            return rows
        hidden = rows.shape[1]
        cut = rows.reshape(self.blocks, hidden, 2, self.block).transpose(1, 2, 0, 3)
        return cut.reshape(1, hidden, self.model)

    def rows_grads(self, near, far, y):
        size = near.shape[-1]
        return self.call(
            rows_grad_kernel,
            [((size // 2, self.model), bf16)] * 2,
            [near, far, *y],
            [pltpu.VMEM((size, self.model), f32)],
        )

    def qkv_grads(self, a, joined):
        shape = ((self.blocks, self.block, 3 * self.width), bf16)
        return self.call(qkv_grad_kernel, [shape] * 2, [*a, joined], micros=4)


def routes(seq_size, group_size, slots_here):
    slots = slots_here * group_size
    parts = seq_size // slots
    result = []
    for r in range(slots_here):
        pairs = []
        for s in range(seq_size):
            for f in range(group_size):
                slot = slots_here * f + (s + r) % slots_here
                t = slot * parts + s // slots
                k = s % slots // slots_here
                pairs.append((s * group_size + f, t * group_size + k))
        result.append(pairs)
    return result


def shards(tokens, doc_bounds, w_qkv, w_out, w_gate, w_up, w_down, norm_attn, norm_mlp, out_grad):
    slots_here, block, model = tokens.shape
    seq_size = lax.axis_size(("sz", "sy"))
    group_size = lax.axis_size(("fx", "fc"))
    sz_size = seq_size // 2
    seq_at = lax.axis_index(("sz", "sy"))
    me = lax.axis_index(("fx", "fc"))
    parts = seq_size // (slots_here * group_size)
    local = slots_here * block
    width = model // group_size
    in_rows = w_qkv.shape[1]
    group_rows = in_rows * group_size
    hidden_rows = w_down.shape[1]
    hidden_here = hidden_rows * seq_size
    paths = routes(seq_size, group_size, slots_here)
    backs = [[(target, source) for source, target in pairs] for pairs in paths]

    def to_group(array):
        got = [
            lax.ppermute(pick(array, (seq_at + r) % 2), ALL, paths[r]) for r in range(slots_here)
        ]
        return in_order(seq_at // parts % 2, got[0], got[1], 0).reshape(local, model)

    def from_group(rows):
        rows = rows.astype(bf16).reshape(slots_here, block, model)
        at = seq_at // parts % 2
        got = [lax.ppermute(pick(rows, (at + r) % 2), ALL, backs[r]) for r in range(slots_here)]
        return in_order(seq_at % 2, got[0], got[1], 0).astype(f32)

    def gathered(own):
        return lax.all_gather(own, "sz", axis=0, tiled=False)

    def qkv_pieces(layer):
        pieces = w_qkv[layer].reshape(in_rows, 3, group_size, width).transpose(2, 0, 1, 3)
        return pieces.reshape(group_size, in_rows, 3 * width)

    def attention_weights(layer, mine):
        outs = w_out[layer].reshape(in_rows, group_size, width).transpose(1, 0, 2)
        own = gathered(jnp.concatenate([mine, outs.reshape(group_rows, width)], axis=1))
        other = swap_y(own[:, :, : 3 * width])
        outs = own[:, :, 3 * width :].reshape(group_size, -1, group_size, in_rows, width)
        outs = exchange(outs.transpose(0, 1, 3, 2, 4).reshape(group_size, -1, in_rows, model))
        outs = outs.transpose(1, 0, 2, 3)
        outs = in_order(group.me_y, outs, swap_y(outs), 1).reshape(width, model)
        return ([own], [other], outs)

    def mlp_weights(layer):
        def cut(weight):
            weight = weight[layer].reshape(in_rows, sz_size, 2, group_size, hidden_rows)
            return weight.transpose(3, 0, 2, 1, 4).reshape(group_size, in_rows, hidden_here)

        mine = exchange(group.hold(jnp.stack([cut(w_gate), cut(w_up)], axis=1)))
        mine = mine.transpose(1, 0, 2, 3).reshape(2 * group_rows, hidden_here).T
        if layer > 0:
            group.need(mine)
        own = gathered(mine)
        return (group.mlp_layout(own), group.mlp_layout(swap_y(own)))

    bounds = lax.ppermute(pick(doc_bounds, seq_at % 2), ALL, paths[0])
    group = Group(local, model, width, parts, bounds)
    gains = jnp.stack([norm_attn[0], norm_mlp[0], norm_attn[1], norm_mlp[1]])
    sums = (to_group(tokens),)
    first_qkv = exchange(qkv_pieces(0)).reshape(group_rows, 3 * width)
    first_qkv, sums = lax.optimization_barrier((first_qkv, sums))
    gains = jnp.stack(by_distance(jnp.stack(gather_near(gains.astype(f32)))))
    gains = gains.transpose(1, 0, 2).reshape(4, sz_size, 1, 1, in_rows)
    gains = in_order(lax.axis_index("fx"), gains, swap_x(gains), 2)[:, :, :, 0]
    gains = in_order(lax.axis_index("fc"), gains, swap_core(gains), 3)
    gains = gains.reshape(4, sz_size * group_rows)
    gains = jnp.concatenate([gains, swap_y(gains)], axis=1)
    gains = [gains[i : i + 1] for i in range(4)]

    attention = [attention_weights(0, first_qkv)]
    mlps, downs = [], None

    valid = group.valid()
    saved = []
    first = None
    for layer in range(LAYERS):
        entry, a = group.norm(sums, gains[2 * layer])
        if layer == 0:
            gates = [mlp_weights(0)]
            downs = gathered(jnp.concatenate([w_down[0], w_down[1]]))
            cut = slice(0, hidden_rows), slice(hidden_rows, 2 * hidden_rows)
            downs = [downs[:, at].reshape(-1, model) for at in cut]
            downs = [(own, swap_y(own)) for own in downs]
            next_qkv = exchange(group.hold(qkv_pieces(1))).reshape(group_rows, 3 * width)
        else:
            group.need(gates[1][0], downs[1][1])
        a = spread(a)
        partial, kept, out, first = group.attend(a, attention[layer], first)
        if layer == 0:
            group.need(next_qkv)
            attention.append(attention_weights(1, next_qkv))
        else:
            group.need(gates[1][1])
        middle, m = group.norm((entry, *group.reduce_pieces(partial)), gains[2 * layer + 1])
        m = spread(m)
        if layer == 0:
            gates.append(mlp_weights(1))
        mlps.append(gates[layer] + downs[layer])
        if layer > 0:
            group.need(*first_up)
        near, far = group.mlp(m, mlps[layer])
        if layer == 0:
            upstream = to_group(group.hold(out_grad)).astype(f32) * valid
            first_up = spread(upstream.astype(bf16))
        if layer == 0:
            group.need(attention[1][1][0], attention[1][2])
        sums = (middle, *group.reduce_pieces((*near[:2], *far[:2])))
        saved.append((entry, a, kept, out, middle, m, near[2:], far[2:]))
    hidden_out = from_group(group.plain_sum(sums) * valid)
    carry = None
    grads = [None] * LAYERS
    gain_grads = [None] * (2 * LAYERS)

    def out_rows(outs):
        if parts == 1:
            rows = group.add(outs[0], outs[1])
        else:
            rows = group.add(*outs)
        rows = rows.reshape(-1, group_size, in_rows, model)
        return exchange(rows.transpose(1, 0, 2, 3)).reshape(sz_size, in_rows, model)

    def swap_outs(keep, send):
        if parts == 1:
            return (keep, swap_y(send))
        both = in_order(group.me_y, keep, send, 0).reshape(-1, 2, group_rows, model)
        return (pick(both, group.me_y, 1), swap_y(pick(both, 1 - group.me_y, 1)))

    def hand_out(layer, pair, down, qkv, rows):
        pair = pair.T.reshape(2, group_size, in_rows, hidden_here).transpose(1, 0, 2, 3)
        pair = exchange(pair)
        pair = pair.reshape(group_size, 2, in_rows, 2, sz_size, hidden_rows)
        pair = pair.transpose(1, 2, 4, 3, 0, 5).reshape(2, in_rows, -1)
        qkv = exchange(qkv.reshape(group_size, in_rows, 3 * width))
        qkv = qkv.reshape(group_size, in_rows, 3, width)
        qkv = qkv.transpose(1, 2, 0, 3).reshape(in_rows, 3 * model)
        grads[layer] = (qkv, rows, pair[0], pair[1], down)

    half = 2 * local
    waiting = None
    for layer in reversed(range(LAYERS)):
        last = layer == 0
        entry, a, kept, out, middle, m, near, far = saved[layer]
        y = first_up if waiting is None else spread(low)
        if waiting is not None:
            pair, qkv, down, outs = waiting
            qkv = scattered(group.add(*qkv))
        near_back, far_back = group.mlp_back(y, (near[:2], far[:2]), mlps[layer])
        if not last:
            group.need(*sums)
        partial = group.reduce_pieces((*near_back[:2], *far_back[:2]))
        keep, send = group.gate_grads(m, near_back[2], far_back[2])
        gate = (keep, swap_y(send))
        if waiting is not None:
            down = group.add(*down).reshape(sz_size, hidden_rows, model)
            rows = scattered(jnp.concatenate([down, out_rows(outs)], axis=1))
        down_keep, down_send = group.rows_grads(near[2], far[2], y)
        upstream, low, gain_grads[2 * layer + 1] = group.norm_back(
            upstream, partial, middle, gains[2 * layer + 1]
        )
        y2 = spread(low)
        keep, send = group.gate_grads(m, near_back[3], far_back[3])
        up = (keep, swap_y(send))
        group.need(gate[1])
        partial, joined, value_grad = group.attend_back(y2, attention[layer], kept, carry, last)
        if not last:
            carry = value_grad if carry is None else carry + value_grad
        partial = group.reduce_pieces(partial)
        keep, send = group.qkv_grads(a, joined)
        qkv_sums = (keep, swap_y(send))
        down_sums = (down_keep, swap_y(down_send))
        if waiting is not None:
            done = [pair, qkv, rows]
        pair = scattered(group.add_pair(gate, up))
        outs = swap_outs(*group.rows_grads(out[:half], out[half:], y2))
        upstream, low, gain_grads[2 * layer] = group.norm_back(
            upstream, partial, entry, gains[2 * layer]
        )
        waiting = (pair, qkv_sums, down_sums, outs)
    pair, qkv, down, outs = waiting
    qkv = scatter_near(by_distance(group.add(*qkv))).astype(bf16)
    down = group.add(*down).reshape(sz_size, hidden_rows, model)
    rows = out_rows(outs)
    extra = sum_near(jnp.concatenate(gain_grads)).reshape(2 * LAYERS, sz_size, group_rows)
    extra = extra.astype(bf16).transpose(1, 0, 2)
    extra = jnp.pad(extra, ((0, 0), (0, 8 - 2 * LAYERS), (0, model - group_rows)))
    rows = scattered(jnp.concatenate([down, rows, extra], axis=1))
    down, rows = rows[:hidden_rows], rows[hidden_rows:]
    gain_sums = rows[in_rows : in_rows + 2 * LAYERS].astype(f32)
    gain_sums = lax.dynamic_slice(gain_sums, (0, me * in_rows), (2 * LAYERS, in_rows))
    pair_1, qkv_1, rows_1 = [group.hold(one) for one in done]
    value_grad = group.hold(value_grad)
    hand_out(1, pair_1, rows_1[:hidden_rows], qkv_1, rows_1[hidden_rows:])
    hand_out(0, pair, down, qkv, rows[:in_rows])
    pieces = value_grad.astype(bf16).reshape(group_size, local, width)
    if parts != 1:
        order = me ^ jnp.arange(group_size, dtype=jnp.int32)
        pieces = jnp.take(pieces, order, axis=0)
    first_grad = exchange(pieces).transpose(1, 0, 2).reshape(local, model)
    stacked = [
        jnp.stack([grads[layer][member].astype(f32) for layer in range(LAYERS)])
        for member in range(5)
    ]
    return (
        hidden_out,
        from_group(upstream),
        *stacked,
        gain_sums[0::2],
        gain_sums[1::2],
        from_group(first_grad),
    )


def solution(mesh):
    seq, fsdp = mesh.shape["seq"], mesh.shape["fsdp"]
    inner = Mesh(mesh.devices.reshape(seq // 2, 2, fsdp // 2, 2), ALL)
    rows = P(("fx", "fc"), ("sz", "sy"), None)
    weight, gain = P(None, ALL, None), P(None, ALL)
    in_specs = (rows, P(("fx", "fc"), None)) + (weight,) * 5 + (gain,) * 2 + (rows,)
    out_specs = (rows, rows) + (weight,) * 5 + (gain,) * 2 + (rows,)
    return jax.shard_map(
        shards, mesh=inner, in_specs=in_specs, out_specs=out_specs, check_vma=False
    )
```

```python
import functools

import jax
import jax.numpy as jnp
from jax import lax
from jax.experimental import pallas as pl
from jax.experimental.pallas import tpu as pltpu
from jax.sharding import Mesh, PartitionSpec as P

HD = 64
LAYERS = 2
epsilon = 1e-05
masked_score = -1e30
SCALE = 0.125 * 1.4426950408889634
bf16 = jnp.bfloat16
f32 = jnp.float32

ALL = ("sz", "sy", "fx", "fc")
SWAP = ((0, 1), (1, 0))
VMEM_LIMIT = 24 * 1024 * 1024


def dot(left, right):
    return jnp.dot(left, right, preferred_element_type=f32)


def dot_rows(left, right):
    return lax.dot_general(left, right, (((0,), (0,)), ((), ())), preferred_element_type=f32)


def dot_cols(left, right):
    return lax.dot_general(left, right, (((1,), (1,)), ((), ())), preferred_element_type=f32)


def swap_core(value):
    return lax.ppermute(value, "fc", SWAP)


def swap_x(value):
    return lax.ppermute(value, "fx", SWAP)


def swap_y(value):
    return lax.ppermute(value, "sy", SWAP)


def pick(array, index, axis=0):
    return lax.dynamic_index_in_dim(array, index, axis, keepdims=False)


def in_order(flag, first, second, axis):
    return jnp.where(
        flag == 0, jnp.stack([first, second], axis), jnp.stack([second, first], axis)
    )


def exchange(pieces):
    fx, fc = lax.axis_index("fx"), lax.axis_index("fc")
    pieces = pieces.reshape((2, 2) + pieces.shape[1:])
    got = swap_x(pick(pieces, 1 - fx))
    both = in_order(fx, pick(pieces, fx), got, 0)
    got = swap_core(pick(both, 1 - fc, 1))
    both = in_order(fc, pick(both, fc, 1), got, 1)
    return both.reshape((4,) + both.shape[2:])


def sum_near(value):
    value = value + swap_x(value)
    value = value + swap_core(value)
    half = value.shape[1] // 2
    got = swap_y(value)
    return value[:, :half] + got[:, half:]


def steps_z():
    size = lax.axis_size("sz")
    return [(d, [(i, i ^ d) for i in range(size)]) for d in range(1, size)]


def gather_near(block):
    return [block] + [lax.ppermute(block, "sz", pairs) for _, pairs in steps_z()]


def scatter_near(blocks):
    total = blocks[0].astype(f32)
    for d, pairs in steps_z():
        total = total + lax.ppermute(blocks[d], "sz", pairs).astype(f32)
    return total


def by_distance(rows):
    at = lax.axis_index("sz")
    return [pick(rows, at ^ d) for d in range(rows.shape[0])]


def scattered(total):
    return lax.psum_scatter(total, "sz", scatter_dimension=0, tiled=False)


def spread(value):
    over = swap_x(value)
    return (value, swap_core(value), over, swap_core(over))


def kernel_call(body, results, scalars, operands, scratch, after, flops):
    count, extra = len(operands), len(after)

    def whole(scalars_ref, *refs):
        body(scalars_ref, *refs[:count], *refs[count + extra :])

    vmem = pl.BlockSpec(memory_space=pltpu.VMEM)
    return pl.pallas_call(
        whole,
        out_shape=[shape_of(*one) for one in results],
        in_specs=[pl.BlockSpec(memory_space=pltpu.SMEM)]
        + [vmem] * count
        + [pl.BlockSpec(memory_space=pl.ANY)] * extra,
        out_specs=[vmem] * len(results),
        scratch_shapes=list(scratch),
        compiler_params=pltpu.CompilerParams(vmem_limit_bytes=VMEM_LIMIT),
        cost_estimate=pl.CostEstimate(
            flops=1, bytes_accessed=1, transcendentals=0
        ),
    )(scalars, *operands, *after)


def shape_of(shape, dtype):
    return jax.ShapeDtypeStruct(shape, dtype)


def block_pairs(scalars, width):
    half, me_y = width // 256, scalars[3]
    for i in range(half):
        yield (i * 128, pl.multiple_of((2 * i + me_y) * 128, 128))
        yield ((half + i) * 128, pl.multiple_of((2 * i + 1 - me_y) * 128, 128))


def norm_kernel(added, scalars, *refs):
    inputs, (gain_ref, sum_ref, out_ref) = refs[:added], refs[added:]
    total = inputs[0][...].astype(f32)
    for ref in inputs[1:]:
        total += (ref[...] if len(ref.shape) == 2 else ref[0]).astype(f32)
    sum_ref[...] = total
    inverse = lax.rsqrt(jnp.mean(total * total, axis=-1, keepdims=True) + epsilon)
    for local, natural in block_pairs(scalars, sum_ref.shape[1]):
        normed = sum_ref[:, pl.ds(natural, 128)] * inverse
        out_ref[:, local : local + 128] = (normed * gain_ref[:, local : local + 128]).astype(bf16)


def norm_back_kernel(scalars, up_ref, d0, d1, d2, z_ref, gain_ref, up_out, low_out, gain_out, work):
    z = z_ref[...]
    inverse = lax.rsqrt(jnp.mean(z * z, axis=-1, keepdims=True) + epsilon)
    for local, natural in block_pairs(scalars, z.shape[1]):
        here = slice(local, local + 128)
        core = d1[:, here] if len(d1.shape) == 2 else d1[0, :, here]
        dy = d0[:, here] + core.astype(f32) + d2[:, here].astype(f32)
        normed = z_ref[:, pl.ds(natural, 128)] * inverse
        gain_out[:, here] = jnp.sum(dy * normed, axis=0, keepdims=True)
        work[:, pl.ds(natural, 128)] = dy * gain_ref[:, here]
    scaled = work[...]
    normed = z * inverse
    mean = jnp.mean(scaled * normed, axis=-1, keepdims=True)
    up = up_ref[...] + inverse * (scaled - normed * mean)
    up_out[...] = up
    low_out[...] = up.astype(bf16)


def add_kernel(scalars, left, right, out_ref):
    out_ref[...] = (left[...].astype(f32) + right[...].astype(f32)).astype(out_ref.dtype)


def add_second_kernel(scalars, left, right, out_ref):
    out_ref[...] = (left[...] + right[1].astype(f32)).astype(out_ref.dtype)


def add_pair_kernel(scalars, left, right, second_left, second_right, out_ref):
    size = left.shape[2]
    out_ref[:, :, :size] = (left[...].astype(f32) + right[...].astype(f32)).astype(bf16)
    out_ref[:, :, size:] = (second_left[...].astype(f32) + second_right[...].astype(f32)).astype(bf16)


def hold_kernel(scalars, value, out_ref):
    out_ref[...] = value[...]


def partner(rows):
    lane = lax.broadcasted_iota(jnp.int32, rows.shape, 1)
    return jnp.where(lane % 64 < 32, pltpu.roll(rows, 96, 1), pltpu.roll(rows, 32, 1))


def block_mask(block, rows, start, end):
    shape = (rows, (block + 1) * rows)
    query = block * rows + lax.broadcasted_iota(jnp.int32, (rows, 1), 0)
    lowest = jnp.where(query < start, 0, jnp.where(query < end, start, end))
    key = lax.broadcasted_iota(jnp.int32, shape, 1)
    return (key <= query) & (key >= lowest)


def weigh_rows(scores, allowed):
    scores = jnp.where(allowed, scores * SCALE, masked_score)
    weights = jnp.exp2(scores - jnp.max(scores, axis=-1, keepdims=True))
    return (weights, 1.0 / jnp.sum(weights, axis=-1, keepdims=True))


def softmax_rows(scores, allowed):
    scores = jnp.where(allowed, scores * 0.125, masked_score)
    weights = jnp.exp(scores - jnp.max(scores, axis=-1, keepdims=True))
    return weights * (1.0 / jnp.sum(weights, axis=-1, keepdims=True))


def flat(ref, first, last):
    value = ref[:, first:last, :]
    return value.reshape(-1, value.shape[-1])


def rows_of(refs, columns):
    values = []
    for ref in refs:
        if len(ref.shape) == 3:
            values.append(ref[:, :, :columns].reshape(-1, columns))
        else:
            values.append(ref[:, :columns])
    return values[0] if len(values) == 1 else jnp.concatenate(values, axis=0)


def place(ref, me_y, own, other):
    half = own.shape[0]
    ref[pl.ds(pl.multiple_of(me_y * half, half), half), :] = own
    ref[pl.ds(pl.multiple_of((1 - me_y) * half, half), half), :] = other


def attention_kernel(blend, count, scalars, a0, a1, a2, a3, *refs):
    own, other, refs = refs[:count], refs[count : 2 * count], refs[2 * count :]
    cos_ref, sin_ref, refs = refs[0], refs[1], refs[2:]
    if blend:
        first_ref, q_ref, k_ref, v_ref, o_ref = refs
    else:
        q_ref, k_ref, v_ref, o_ref, first_ref = refs
    me, start, end = scalars[0], scalars[1], scalars[2]
    total, width = q_ref.shape
    rows = total // 4
    here_w, there_w = rows_of(own, 3 * width), rows_of(other, 3 * width)
    half = here_w.shape[0]
    for i, a_ref in enumerate((a0, a1, a2, a3)):
        part = dot(a_ref[:, :half], here_w) + dot(a_ref[:, half:], there_w)
        here = slice(i * rows, (i + 1) * rows)
        there = pl.ds(pl.multiple_of((me ^ i) * rows, rows), rows)
        cosine, sine = cos_ref[here, :], sin_ref[here, :]
        for j in range(width // 128):
            for into, at in ((q_ref, 0), (k_ref, width)):
                piece = part[:, at + j * 128 : at + (j + 1) * 128]
                turned = piece * cosine + partner(piece) * sine
                into[there, j * 128 : (j + 1) * 128] = turned.astype(bf16)
        value = part[:, 2 * width :]
        if blend:
            value = 0.5 * value + 0.5 * first_ref[there, :]
        else:
            first_ref[there, :] = value
        v_ref[there, :] = value.astype(bf16)
    lane = lax.broadcasted_iota(jnp.int32, (rows, 128), 1)
    for b in range(4):
        allowed = block_mask(b, rows, start, end)
        there = pl.ds(pl.multiple_of((me ^ b) * rows, rows), rows)
        for j in range(width // 128):
            columns = slice(j * 128, (j + 1) * 128)
            query = q_ref[b * rows : (b + 1) * rows, columns]
            keys = k_ref[: (b + 1) * rows, columns]
            values = v_ref[: (b + 1) * rows, columns]
            outs = []
            for h in range(2):
                one = jnp.where(lane // 64 == h, query, jnp.zeros_like(query))
                weights, share = weigh_rows(dot_cols(one, keys), allowed)
                outs.append(dot(weights.astype(bf16), values) * share)
            o_ref[there, columns] = jnp.where(lane < 64, outs[0], outs[1]).astype(bf16)


def out_kernel(scalars, o_ref, out_w, near, far, cores):
    rows = near.shape[0]
    cores[1] = dot(o_ref[3 * rows :, :], out_w[...]).astype(bf16)
    cores[0] = dot(o_ref[rows : 2 * rows, :], out_w[...]).astype(bf16)
    far[...] = dot(o_ref[2 * rows : 3 * rows, :], out_w[...])
    near[...] = dot(o_ref[:rows, :], out_w[...])


def attention_back_kernel(last, count, scalars, y0, y1, y2, y3, *refs):
    own, other, refs = refs[:count], refs[count : 2 * count], refs[2 * count :]
    out_w, cos_ref, sin_ref, q_ref, k_ref, v_ref = refs[:6]
    refs = refs[6:]
    if last:
        carry_ref, near, far, cores, d_ref, dv_ref, dk_sum, dv_sum, up_ref = refs
    else:
        near, far, cores, d_ref, dv_ref, dk_sum, dv_sum, up_ref = refs
    me, start, end = scalars[0], scalars[1], scalars[2]
    total, width = q_ref.shape
    rows = total // 4
    for i, y_ref in enumerate((y0, y1, y2, y3)):
        there = pl.ds(pl.multiple_of((me ^ i) * rows, rows), rows)
        up_ref[there, :] = dot_cols(y_ref[...], out_w[...]).astype(bf16)
    lane = lax.broadcasted_iota(jnp.int32, (rows, 128), 1)
    dk_sum[...] = jnp.zeros_like(dk_sum)
    dv_sum[...] = jnp.zeros_like(dv_sum)
    for b in range(4):
        allowed = block_mask(b, rows, start, end)
        there = pl.ds(pl.multiple_of((me ^ b) * rows, rows), rows)
        upto = slice(0, (b + 1) * rows)
        cosine, sine = cos_ref[there, :], sin_ref[there, :]
        for j in range(width // 128):
            columns = slice(j * 128, (j + 1) * 128)
            query = q_ref[b * rows : (b + 1) * rows, columns]
            keys, values = k_ref[upto, columns], v_ref[upto, columns]
            up = up_ref[b * rows : (b + 1) * rows, columns]
            dq, dk, dv = [], [], []
            for h in range(2):
                mine = lane // 64 == h
                one = jnp.where(mine, query, jnp.zeros_like(query))
                one_up = jnp.where(mine, up, jnp.zeros_like(up))
                weights, share = weigh_rows(dot_cols(one, keys), allowed)
                chance = weights * share
                back = dot_cols(one_up, values)
                delta = jnp.sum(chance * back, axis=-1, keepdims=True)
                score = (chance * (back - delta)).astype(bf16)
                dq.append(dot(score, keys))
                dk.append(dot_rows(score, one * 0.125))
                dv.append(dot_rows(chance.astype(bf16), one_up))
            dk_sum[upto, columns] += dk[0] + dk[1]
            dv_sum[upto, columns] += dv[0] + dv[1]
            dq = jnp.where(lane < 64, dq[0], dq[1]) * 0.125
            d_ref[there, columns] = (dq * cosine - partner(dq) * sine).astype(bf16)
    for b in range(4):
        there = pl.ds(pl.multiple_of((me ^ b) * rows, rows), rows)
        here = slice(b * rows, (b + 1) * rows)
        cosine, sine = cos_ref[there, :], sin_ref[there, :]
        for j in range(width // 128):
            dk = dk_sum[here, j * 128 : (j + 1) * 128]
            dk = dk * cosine - partner(dk) * sine
            d_ref[there, width + j * 128 : width + (j + 1) * 128] = dk.astype(bf16)
        dv = dv_sum[here, :]
        dv = dv + carry_ref[here, :] if last else 0.5 * dv
        dv_ref[here, :] = dv
        d_ref[there, 2 * width : 3 * width] = dv.astype(bf16)
    here_w, there_w = rows_of(own, 3 * width), rows_of(other, 3 * width)
    half = here_w.shape[0]
    for at, weight in ((slice(0, half), here_w), (slice(half, 2 * half), there_w)):
        for i in range(4):
            total_d = dot_cols(d_ref[i * rows : (i + 1) * rows, :], weight)
            if i % 2:
                cores[i // 2, :, at] = total_d.astype(bf16)
            else:
                (far if i else near)[:, at] = total_d


def mlp_halves(ref):
    size = ref.shape[2] // 2
    blocks = range(ref.shape[0])
    return [
        jnp.concatenate([ref[z, :, at : at + size] for z in blocks], axis=1) for at in (0, size)
    ]


def mlp_kernel(scalars, m0, m1, own, other, down_own, down_other, p0, p1, g_ref, u_ref, z_ref, down):
    rows = m0.shape[0]
    place(down, scalars[3], down_own[...], down_other[...])
    gate_own, up_own = mlp_halves(own)
    gate_other, up_other = mlp_halves(other)
    half = gate_own.shape[1]
    for i, (m_ref, p_ref) in enumerate(((m0, p0), (m1, p1))):
        here = slice(i * rows, (i + 1) * rows)
        left, right = m_ref[:, :half], m_ref[:, half:]
        gate = dot_cols(left, gate_own) + dot_cols(right, gate_other)
        up = dot_cols(left, up_own) + dot_cols(right, up_other)
        active = (jax.nn.silu(gate) * up).astype(bf16)
        g_ref[here, :] = gate.astype(bf16)
        u_ref[here, :] = up.astype(bf16)
        z_ref[here, :] = active
        p_ref[...] = dot(active, down[...]).astype(p_ref.dtype)


def mlp_back_kernel(scalars, y0, y1, g_ref, u_ref, own, other, down_own, down_other, p0, p1, dg_ref, du_ref, down):
    rows = y0.shape[0]
    place(down, scalars[3], down_own[...], down_other[...])
    gate_own, up_own = mlp_halves(own)
    gate_other, up_other = mlp_halves(other)
    half = gate_own.shape[1]
    for i, (y_ref, p_ref) in enumerate(((y0, p0), (y1, p1))):
        here = slice(i * rows, (i + 1) * rows)
        back = dot_cols(y_ref[...], down[...])
        gate, up = g_ref[here, :].astype(f32), u_ref[here, :].astype(f32)
        sigmoid = jax.nn.sigmoid(gate)
        dg = (back * up * sigmoid * (1.0 + gate * (1.0 - sigmoid))).astype(bf16)
        du = (back * (gate * sigmoid)).astype(bf16)
        dg_ref[here, :] = dg
        du_ref[here, :] = du
        p_ref[:, :half] = (dot(dg, gate_own) + dot(du, up_own)).astype(p_ref.dtype)
        p_ref[:, half:] = (dot(dg, gate_other) + dot(du, up_other)).astype(p_ref.dtype)


def gate_grad_kernel(scalars, m0, m1, m2, m3, near, far, keep, send):
    rows = m0.shape[0]
    blocks, size = keep.shape[0], keep.shape[2]
    half = blocks * size
    for into, columns in ((send, slice(half, 2 * half)), (keep, slice(0, half))):
        total = dot_rows(near[:rows, :], m0[:, columns])
        total += dot_rows(near[rows:, :], m1[:, columns])
        total += dot_rows(far[:rows, :], m2[:, columns])
        total += dot_rows(far[rows:, :], m3[:, columns])
        for z in range(blocks):
            into[z] = total[:, z * size : (z + 1) * size].astype(bf16)


def rows_grad_kernel(scalars, left_near, left_far, y0, y1, y2, y3, keep, send, work):
    rows = y0.shape[0]
    half = keep.shape[0]
    work[...] = dot_rows(left_near[:rows, :], y0[...]) + dot_rows(left_near[rows:, :], y1[...])
    work[...] += dot_rows(left_far[:rows, :], y2[...]) + dot_rows(left_far[rows:, :], y3[...])
    me_y = scalars[3]
    keep[...] = work[pl.ds(pl.multiple_of(me_y * half, half), half), :].astype(bf16)
    send[...] = work[pl.ds(pl.multiple_of((1 - me_y) * half, half), half), :].astype(bf16)


def qkv_grad_kernel(scalars, a0, a1, a2, a3, d_ref, keep, send):
    rows = a0.shape[0]
    blocks, size = keep.shape[0], keep.shape[1]
    half = blocks * size
    for into, columns in ((send, slice(half, 2 * half)), (keep, slice(0, half))):
        total = dot_rows(a0[:, columns], d_ref[:rows, :])
        for i, a_ref in ((1, a1), (2, a2), (3, a3)):
            total += dot_rows(a_ref[:, columns], d_ref[i * rows : (i + 1) * rows, :])
        into[...] = total.astype(bf16).reshape(blocks, size, -1)


def turn(rows, cosine, sine):
    total, width = rows.shape
    halves = rows.reshape(total, width // HD, 2, HD // 2)
    cosine = cosine[:, :HD].reshape(total, 1, 2, HD // 2)
    sine = sine[:, :HD].reshape(total, 1, 2, HD // 2)
    return (halves * cosine + halves[:, :, ::-1] * sine).reshape(total, width)


class Group:
    def __init__(self, local, model, width, parts, bounds):
        self.local, self.model, self.width, self.parts = local, model, width, parts
        self.total = total = 4 * local
        self.me_y = lax.axis_index("sy")
        self.blocks = lax.axis_size("sz")
        me = lax.axis_index(("fx", "fc"))
        self.part = lax.axis_index(("sz", "sy")) % parts
        order = (me ^ jnp.arange(4, dtype=jnp.int32)) * local
        self.inner = (order[:, None] + jnp.arange(local, dtype=jnp.int32)[None, :]).reshape(total)
        self.start, self.end = bounds[0], bounds[1]
        self.index = index = self.part * total + self.inner
        self.me_z = lax.axis_index("sz")
        self.scalars = jnp.stack([me, self.start, self.end, self.me_y, self.me_z]).astype(jnp.int32)
        base = jnp.where(index < self.start, 0, jnp.where(index < self.end, self.start, self.end))
        frequency = 10000.0 ** (-jnp.arange(HD // 2, dtype=f32) * 2.0 / HD)
        angles = (index - base).astype(f32)[:, None] * frequency[None, :]
        cosine, sine = jnp.cos(angles), jnp.sin(angles)
        self.cosine = jnp.concatenate([cosine] * 4, axis=1)
        self.sine = jnp.concatenate([-sine, sine] * 2, axis=1)
        self.block = model // (2 * self.blocks)
        self.latest, self.needed = None, []

    def call(self, body, shapes, operands, scratch=(), micros=1):
        after = self.needed + ([] if self.latest is None else [self.latest])
        self.needed = []
        flops = int(micros * 1e9)
        got = kernel_call(body, shapes, self.scalars, operands, scratch, after, flops)
        self.latest = got[-1]
        return got

    def add(self, left, right):
        return self.call(add_kernel, [(left.shape, bf16)], [left, right])[0]

    def need(self, *values):
        self.needed += values

    def add_pair(self, first, second):
        shape = (*first[0].shape[:2], 2 * first[0].shape[2])
        if self.block % 128:
            sums = [self.add(*one) for one in (first, second)]
            return jnp.concatenate(sums, axis=2)
        return self.call(add_pair_kernel, [(shape, bf16)], [*first, *second])[0]

    def hold(self, value):
        return self.call(hold_kernel, [(value.shape, value.dtype)], [value])[0]

    def reduce_pieces(self, pieces):
        if len(pieces) == 3:
            got = swap_core(pieces[2])
            out = self.call(
                add_second_kernel,
                [(pieces[1].shape, bf16)],
                [pieces[1], got],
            )[0]
            return (pieces[0], got, swap_x(out))
        got = swap_core(pieces[3])
        out = self.call(
            add_kernel, [(got.shape, bf16)], [pieces[2], got]
        )[0]
        return (pieces[0], swap_core(pieces[1]), swap_x(out))

    def sum_y(self, keep, send):
        return self.add(keep, send)

    def valid(self):
        return (self.index[: self.local] < self.end).astype(f32)[:, None]

    def to_local(self, rows):
        cut = rows.reshape(rows.shape[0], self.blocks, 2, self.block)
        pair = in_order(self.me_y, cut[:, :, 0], cut[:, :, 1], 1)
        return pair.reshape(rows.shape[0], self.model)

    def to_natural(self, rows):
        cut = rows.reshape(rows.shape[0], 2, self.blocks, self.block)
        cut = in_order(self.me_y, cut[:, 0], cut[:, 1], 2)
        return cut.reshape(rows.shape[0], self.model)

    def plain_sum(self, pieces):
        return sum((one if one.ndim == 2 else one[0]).astype(f32) for one in pieces)

    def norm(self, pieces, gain):
        if self.block % 128 == 0:
            shape = (self.local, self.model)
            return self.call(
                functools.partial(norm_kernel, len(pieces)),
                [(shape, f32), (shape, bf16)],
                [*pieces, gain],
            )
        total = self.plain_sum(pieces)
        inverse = lax.rsqrt(jnp.mean(total * total, axis=-1, keepdims=True) + epsilon)
        return (total, (self.to_local(total * inverse) * gain).astype(bf16))

    def norm_back(self, up, pieces, z, gain):
        if self.block % 128 == 0:
            shape = (self.local, self.model)
            return self.call(
                norm_back_kernel,
                [(shape, f32), (shape, bf16), ((1, self.model), f32)],
                [up, *pieces, z, gain],
                [pltpu.VMEM(shape, f32)],
            )
        dy = self.plain_sum(pieces)
        inverse = lax.rsqrt(jnp.mean(z * z, axis=-1, keepdims=True) + epsilon)
        normed = z * inverse
        gain_grad = jnp.sum(dy * self.to_local(normed), axis=0, keepdims=True)
        scaled = self.to_natural(dy * gain)
        mean = jnp.mean(scaled * normed, axis=-1, keepdims=True)
        up = up + inverse * (scaled - normed * mean)
        return (up, up.astype(bf16), gain_grad)

    def pieces(self):
        shape = (self.local, self.model)
        return [(shape, f32), (shape, f32), ((2, *shape), bf16)]

    def cut(self, rows):
        cut = rows.reshape(4, self.local, -1)
        return (cut[0], cut[2], cut[1::2].astype(bf16))

    def attend(self, a, weights, first):
        total, width = self.total, self.width
        tables = [self.cosine, self.sine]
        own, other, out_w = weights
        if self.parts == 1:
            results = [((total, width), bf16)] * 4
            operands = [*a, *own, *other, *tables]
            if first is None:
                results += [((total, width), f32)]
            else:
                operands += [first]
            got = self.call(
                functools.partial(attention_kernel, first is not None, len(own)),
                results,
                operands,
                micros=12,
            )
            partial = self.call(out_kernel, self.pieces(), [got[3], out_w], micros=3)
            return (partial, got[:3], got[3], got[4] if first is None else first)
        own, other = self.plain(own), self.plain(other)
        rows = jnp.concatenate(a)
        part = dot(rows[:, : own.shape[0]], own) + dot(rows[:, own.shape[0] :], other)
        query = turn(part[:, :width], *tables).astype(bf16)
        key = turn(part[:, width : 2 * width], *tables).astype(bf16)
        value = part[:, 2 * width :]
        if first is None:
            first = value
        else:
            value = 0.5 * value + 0.5 * first
        value = value.astype(bf16)

        def one(items):
            q, k, v = items
            return dot(softmax_rows(dot_cols(q, k), self.allowed()).astype(bf16), v)

        packed = (self.heads(query), self.heads(self.slot(key)), self.heads(self.slot(value)))
        out = self.rows(lax.map(one, packed)).astype(bf16)
        return (self.cut(dot(out, out_w)), (query, key, value), out, first)

    def attend_back(self, y, weights, saved, carry, last):
        total, width = self.total, self.width
        own, other, out_w = weights
        if self.parts == 1:
            operands = [*y, *own, *other, out_w, self.cosine, self.sine, *saved]
            if last:
                operands += [carry]
            got = self.call(
                functools.partial(attention_back_kernel, last, len(own)),
                self.pieces() + [((total, 3 * width), bf16), ((total, width), f32)],
                operands,
                [pltpu.VMEM((total, width), f32)] * 2 + [pltpu.VMEM((total, width), bf16)],
                micros=20,
            )
            return (got[:3], got[3], got[4])
        own, other = self.plain(own), self.plain(other)
        query, key, value = saved
        up = dot_cols(jnp.concatenate(y), out_w).astype(bf16)

        def one(items):
            q, k, v, u = items
            chance = softmax_rows(dot_cols(q, k), self.allowed())
            back = dot_cols(u, v)
            delta = jnp.sum(chance * back, axis=-1, keepdims=True)
            score = (chance * (back - delta) * 0.125).astype(bf16)
            return (dot(score, k), dot_rows(score, q), dot_rows(chance.astype(bf16), u))

        packed = (query, self.slot(key), self.slot(value), up)
        dq, dk, dv = lax.map(one, tuple(self.heads(rows) for rows in packed))
        dk, dv = self.collect(self.rows(dk)), self.collect(self.rows(dv))
        dv = dv + carry if last else 0.5 * dv
        back_turn = functools.partial(turn, cosine=self.cosine, sine=-self.sine)
        joined = jnp.concatenate([back_turn(self.rows(dq)), back_turn(dk), dv], axis=1)
        joined = joined.astype(bf16)
        sums = jnp.concatenate([dot_cols(joined, own), dot_cols(joined, other)], axis=1)
        return (self.cut(sums), joined, dv)

    def plain(self, blocks):
        wide = 3 * self.width
        return jnp.concatenate([block[..., :wide].reshape(-1, wide) for block in blocks])

    def rotate_parts(self, value, shift):
        if shift % self.parts == 0:
            return value
        pairs = []
        for t in range(lax.axis_size(("sz", "sy"))):
            head = t - t % self.parts
            pairs.append((head + (t + shift) % self.parts, t))
        return lax.ppermute(value, ("sz", "sy"), pairs)

    def slot(self, value):
        return jnp.concatenate([self.rotate_parts(value, r) for r in range(self.parts)])

    def heads(self, rows):
        return rows.reshape(rows.shape[0], -1, HD).transpose(1, 0, 2)

    def rows(self, heads):
        return heads.transpose(1, 0, 2).reshape(heads.shape[1], -1)

    def allowed(self):
        key = jnp.concatenate(
            [(self.part + r) % self.parts * self.total + self.inner for r in range(self.parts)]
        )
        query = self.index[:, None]
        lowest = jnp.where(
            query < self.start, 0, jnp.where(query < self.end, self.start, self.end)
        )
        return (key[None, :] <= query) & (key[None, :] >= lowest)

    def collect(self, slot_rows):
        pieces = slot_rows.reshape(self.parts, self.total, -1)
        result = pieces[0]
        for r in range(1, self.parts):
            result = result + self.rotate_parts(pieces[r].astype(bf16), -r).astype(f32)
        return result

    def mlp(self, m, weights):
        hidden = weights[0].shape[1]
        rows = 2 * self.local
        shape = (self.local, self.model)
        scratch = [pltpu.VMEM((hidden, self.model), bf16)]
        results = [(shape, f32), (shape, bf16)] + [((rows, hidden), bf16)] * 3
        return [
            self.call(mlp_kernel, results, [*pair, *weights], scratch, 6)
            for pair in (m[:2], m[2:])
        ]

    def mlp_back(self, y, saved, weights):
        hidden = weights[0].shape[1]
        rows = 2 * self.local
        shape = (self.local, self.model)
        scratch = [pltpu.VMEM((hidden, self.model), bf16)]
        results = [(shape, f32), (shape, bf16)] + [((rows, hidden), bf16)] * 2
        return [
            self.call(mlp_back_kernel, results, [*pair, *kept, *weights], scratch, 6)
            for pair, kept in ((y[:2], saved[0]), (y[2:], saved[1]))
        ]

    def gate_grads(self, m, near, far):
        hidden = near.shape[-1]
        blocks = self.blocks if self.block % 128 == 0 else 1
        shape = ((blocks, hidden, self.model // 2 // blocks), bf16)
        keep, send = self.call(
            gate_grad_kernel,
            [shape] * 2,
            [*m, near, far],
        )
        if blocks != self.blocks:
            keep, send = [
                rows.reshape(hidden, self.blocks, self.block).transpose(1, 0, 2)
                for rows in (keep, send)
            ]
        return (keep, send)

    def mlp_layout(self, rows):
        if self.block % 128 == 0:
            return rows
        hidden = rows.shape[1]
        cut = rows.reshape(self.blocks, hidden, 2, self.block).transpose(1, 2, 0, 3)
        return cut.reshape(1, hidden, self.model)

    def rows_grads(self, near, far, y):
        size = near.shape[-1]
        return self.call(
            rows_grad_kernel,
            [((size // 2, self.model), bf16)] * 2,
            [near, far, *y],
            [pltpu.VMEM((size, self.model), f32)],
        )

    def qkv_grads(self, a, joined):
        shape = ((self.blocks, self.block, 3 * self.width), bf16)
        return self.call(qkv_grad_kernel, [shape] * 2, [*a, joined], micros=4)


def routes(seq_size, group_size, slots_here):
    slots = slots_here * group_size
    parts = seq_size // slots
    result = []
    for r in range(slots_here):
        pairs = []
        for s in range(seq_size):
            for f in range(group_size):
                slot = slots_here * f + (s + r) % slots_here
                t = slot * parts + s // slots
                k = s % slots // slots_here
                pairs.append((s * group_size + f, t * group_size + k))
        result.append(pairs)
    return result


def shards(tokens, doc_bounds, w_qkv, w_out, w_gate, w_up, w_down, norm_attn, norm_mlp, out_grad):
    slots_here, block, model = tokens.shape
    seq_size = lax.axis_size(("sz", "sy"))
    group_size = lax.axis_size(("fx", "fc"))
    sz_size = seq_size // 2
    seq_at = lax.axis_index(("sz", "sy"))
    me = lax.axis_index(("fx", "fc"))
    parts = seq_size // (slots_here * group_size)
    local = slots_here * block
    width = model // group_size
    in_rows = w_qkv.shape[1]
    group_rows = in_rows * group_size
    hidden_rows = w_down.shape[1]
    hidden_here = hidden_rows * seq_size
    paths = routes(seq_size, group_size, slots_here)
    backs = [[(target, source) for source, target in pairs] for pairs in paths]

    def to_group(array):
        got = [
            lax.ppermute(pick(array, (seq_at + r) % 2), ALL, paths[r]) for r in range(slots_here)
        ]
        return in_order(seq_at // parts % 2, got[0], got[1], 0).reshape(local, model)

    def from_group(rows):
        rows = rows.astype(bf16).reshape(slots_here, block, model)
        at = seq_at // parts % 2
        got = [lax.ppermute(pick(rows, (at + r) % 2), ALL, backs[r]) for r in range(slots_here)]
        return in_order(seq_at % 2, got[0], got[1], 0).astype(f32)

    def gathered(own):
        return lax.all_gather(own, "sz", axis=0, tiled=False)

    def qkv_pieces(layer):
        pieces = w_qkv[layer].reshape(in_rows, 3, group_size, width).transpose(2, 0, 1, 3)
        return pieces.reshape(group_size, in_rows, 3 * width)

    def attention_weights(layer, mine):
        outs = w_out[layer].reshape(in_rows, group_size, width).transpose(1, 0, 2)
        own = gathered(jnp.concatenate([mine, outs.reshape(group_rows, width)], axis=1))
        other = swap_y(own[:, :, : 3 * width])
        outs = own[:, :, 3 * width :].reshape(group_size, -1, group_size, in_rows, width)
        outs = exchange(outs.transpose(0, 1, 3, 2, 4).reshape(group_size, -1, in_rows, model))
        outs = outs.transpose(1, 0, 2, 3)
        outs = in_order(group.me_y, outs, swap_y(outs), 1).reshape(width, model)
        return ([own], [other], outs)

    def mlp_weights(layer):
        def cut(weight):
            weight = weight[layer].reshape(in_rows, sz_size, 2, group_size, hidden_rows)
            return weight.transpose(3, 0, 2, 1, 4).reshape(group_size, in_rows, hidden_here)

        mine = exchange(group.hold(jnp.stack([cut(w_gate), cut(w_up)], axis=1)))
        mine = mine.transpose(1, 0, 2, 3).reshape(2 * group_rows, hidden_here).T
        if layer > 0:
            group.need(mine)
        own = gathered(mine)
        return (group.mlp_layout(own), group.mlp_layout(swap_y(own)))

    bounds = lax.ppermute(pick(doc_bounds, seq_at % 2), ALL, paths[0])
    group = Group(local, model, width, parts, bounds)
    gains = jnp.stack([norm_attn[0], norm_mlp[0], norm_attn[1], norm_mlp[1]])
    sums = (to_group(tokens),)
    first_qkv = exchange(qkv_pieces(0)).reshape(group_rows, 3 * width)
    first_qkv, sums = lax.optimization_barrier((first_qkv, sums))
    gains = jnp.stack(by_distance(jnp.stack(gather_near(gains.astype(f32)))))
    gains = gains.transpose(1, 0, 2).reshape(4, sz_size, 1, 1, in_rows)
    gains = in_order(lax.axis_index("fx"), gains, swap_x(gains), 2)[:, :, :, 0]
    gains = in_order(lax.axis_index("fc"), gains, swap_core(gains), 3)
    gains = gains.reshape(4, sz_size * group_rows)
    gains = jnp.concatenate([gains, swap_y(gains)], axis=1)
    gains = [gains[i : i + 1] for i in range(4)]

    attention = [attention_weights(0, first_qkv)]
    mlps, downs = [], None

    valid = group.valid()
    saved = []
    first = None
    for layer in range(LAYERS):
        entry, a = group.norm(sums, gains[2 * layer])
        if layer == 0:
            gates = [mlp_weights(0)]
            downs = gathered(jnp.concatenate([w_down[0], w_down[1]]))
            cut = slice(0, hidden_rows), slice(hidden_rows, 2 * hidden_rows)
            downs = [downs[:, at].reshape(-1, model) for at in cut]
            downs = [(own, swap_y(own)) for own in downs]
            next_qkv = exchange(group.hold(qkv_pieces(1))).reshape(group_rows, 3 * width)
        else:
            group.need(gates[1][0], downs[1][1])
        a = spread(a)
        partial, kept, out, first = group.attend(a, attention[layer], first)
        if layer == 0:
            group.need(next_qkv)
            attention.append(attention_weights(1, next_qkv))
        else:
            group.need(gates[1][1])
        middle, m = group.norm((entry, *group.reduce_pieces(partial)), gains[2 * layer + 1])
        m = spread(m)
        if layer == 0:
            gates.append(mlp_weights(1))
        mlps.append(gates[layer] + downs[layer])
        if layer > 0:
            group.need(*first_up)
        near, far = group.mlp(m, mlps[layer])
        if layer == 0:
            upstream = to_group(group.hold(out_grad)).astype(f32) * valid
            first_up = spread(upstream.astype(bf16))
        if layer == 0:
            group.need(attention[1][1][0], attention[1][2])
        sums = (middle, *group.reduce_pieces((*near[:2], *far[:2])))
        saved.append((entry, a, kept, out, middle, m, near[2:], far[2:]))
    hidden_out = from_group(group.plain_sum(sums) * valid)
    carry = None
    grads = [None] * LAYERS
    gain_grads = [None] * (2 * LAYERS)

    def out_rows(outs):
        if parts == 1:
            rows = group.add(outs[0], outs[1])
        else:
            rows = group.add(*outs)
        rows = rows.reshape(-1, group_size, in_rows, model)
        return exchange(rows.transpose(1, 0, 2, 3)).reshape(sz_size, in_rows, model)

    def swap_outs(keep, send):
        if parts == 1:
            return (keep, swap_y(send))
        both = in_order(group.me_y, keep, send, 0).reshape(-1, 2, group_rows, model)
        return (pick(both, group.me_y, 1), swap_y(pick(both, 1 - group.me_y, 1)))

    def hand_out(layer, pair, down, qkv, rows):
        pair = pair.T.reshape(2, group_size, in_rows, hidden_here).transpose(1, 0, 2, 3)
        pair = exchange(pair)
        pair = pair.reshape(group_size, 2, in_rows, 2, sz_size, hidden_rows)
        pair = pair.transpose(1, 2, 4, 3, 0, 5).reshape(2, in_rows, -1)
        qkv = exchange(qkv.reshape(group_size, in_rows, 3 * width))
        qkv = qkv.reshape(group_size, in_rows, 3, width)
        qkv = qkv.transpose(1, 2, 0, 3).reshape(in_rows, 3 * model)
        grads[layer] = (qkv, rows, pair[0], pair[1], down)

    half = 2 * local
    waiting = None
    for layer in reversed(range(LAYERS)):
        last = layer == 0
        entry, a, kept, out, middle, m, near, far = saved[layer]
        y = first_up if waiting is None else spread(low)
        if waiting is not None:
            pair, qkv, down, outs = waiting
            qkv = scattered(group.add(*qkv))
        near_back, far_back = group.mlp_back(y, (near[:2], far[:2]), mlps[layer])
        if not last:
            group.need(*sums)
        partial = group.reduce_pieces((*near_back[:2], *far_back[:2]))
        keep, send = group.gate_grads(m, near_back[2], far_back[2])
        gate = (keep, swap_y(send))
        if waiting is not None:
            down = group.add(*down).reshape(sz_size, hidden_rows, model)
            rows = scattered(jnp.concatenate([down, out_rows(outs)], axis=1))
        down_keep, down_send = group.rows_grads(near[2], far[2], y)
        upstream, low, gain_grads[2 * layer + 1] = group.norm_back(
            upstream, partial, middle, gains[2 * layer + 1]
        )
        y2 = spread(low)
        keep, send = group.gate_grads(m, near_back[3], far_back[3])
        up = (keep, swap_y(send))
        group.need(gate[1])
        partial, joined, value_grad = group.attend_back(y2, attention[layer], kept, carry, last)
        if not last:
            carry = value_grad if carry is None else carry + value_grad
        partial = group.reduce_pieces(partial)
        keep, send = group.qkv_grads(a, joined)
        qkv_sums = (keep, swap_y(send))
        down_sums = (down_keep, swap_y(down_send))
        if waiting is not None:
            done = [pair, qkv, rows]
        pair = scattered(group.add_pair(gate, up))
        outs = swap_outs(*group.rows_grads(out[:half], out[half:], y2))
        upstream, low, gain_grads[2 * layer] = group.norm_back(
            upstream, partial, entry, gains[2 * layer]
        )
        waiting = (pair, qkv_sums, down_sums, outs)
    pair, qkv, down, outs = waiting
    qkv = scatter_near(by_distance(group.add(*qkv))).astype(bf16)
    down = group.add(*down).reshape(sz_size, hidden_rows, model)
    rows = out_rows(outs)
    extra = sum_near(jnp.concatenate(gain_grads)).reshape(2 * LAYERS, sz_size, group_rows)
    extra = extra.astype(bf16).transpose(1, 0, 2)
    extra = jnp.pad(extra, ((0, 0), (0, 8 - 2 * LAYERS), (0, model - group_rows)))
    rows = scattered(jnp.concatenate([down, rows, extra], axis=1))
    down, rows = rows[:hidden_rows], rows[hidden_rows:]
    gain_sums = rows[in_rows : in_rows + 2 * LAYERS].astype(f32)
    gain_sums = lax.dynamic_slice(gain_sums, (0, me * in_rows), (2 * LAYERS, in_rows))
    pair_1, qkv_1, rows_1 = [group.hold(one) for one in done]
    hand_out(1, pair_1, rows_1[:hidden_rows], qkv_1, rows_1[hidden_rows:])
    hand_out(0, pair, down, qkv, rows[:in_rows])
    pieces = value_grad.astype(bf16).reshape(group_size, local, width)
    if parts != 1:
        order = me ^ jnp.arange(group_size, dtype=jnp.int32)
        pieces = jnp.take(pieces, order, axis=0)
    first_grad = exchange(pieces).transpose(1, 0, 2).reshape(local, model)
    stacked = [
        jnp.stack([grads[layer][member].astype(f32) for layer in range(LAYERS)])
        for member in range(5)
    ]
    return (
        hidden_out,
        from_group(upstream),
        *stacked,
        gain_sums[0::2],
        gain_sums[1::2],
        from_group(first_grad),
    )


def solution(mesh):
    seq, fsdp = mesh.shape["seq"], mesh.shape["fsdp"]
    inner = Mesh(mesh.devices.reshape(seq // 2, 2, fsdp // 2, 2), ALL)
    rows = P(("fx", "fc"), ("sz", "sy"), None)
    weight, gain = P(None, ALL, None), P(None, ALL)
    in_specs = (rows, P(("fx", "fc"), None)) + (weight,) * 5 + (gain,) * 2 + (rows,)
    out_specs = (rows, rows) + (weight,) * 5 + (gain,) * 2 + (rows,)
    return jax.shard_map(
        shards, mesh=inner, in_specs=in_specs, out_specs=out_specs, check_vma=False
    )
```
